768 devices in a mesh: outer: 32 (over y_hi, x, core), inner: 24 (over z, y_lo).
Axes of the slice: x: 4, y: 8 (y_hi: 4, y_lo: 2; y = y_hi * 2 + y_lo), z: 12, core: 2. Of those that a mesh axis runs over, the one named last changes fastest.
Arguments:
- images: bfloat16 [12288, 1152], P(('outer', 'inner')), as said below
- texts: bfloat16 [98304, 1152], P(('outer', 'inner')), as said below
- logit_scale: float32 [1], replicated, may hold values from 8 to 20
- logit_bias: float32 [1], replicated, may hold values from -2 to 0
Outputs:
- grad_images: float32 [12288, 1152], P(('outer', 'inner'))
- grad_texts: float32 [98304, 1152], P(('outer', 'inner'))
The draws below stay inside these ranges and needn't reach their ends.
Inputs may be any that keep to these rules, and one draw needn't show every extreme that they name: `images`: entries are finite. `texts`: entries are finite.
All inputs are finite; a program needn't handle non-finite values.
Results may differ from the reference program's by a relative error of at most 0.002.
Values may be sent and summed in bfloat16 or wider, within the bound.
A program may use at most 32 MiB of HBM per device.

```python
import math
import jax
import jax.numpy as jnp
from jax import lax

D = 1152
TXT_DEV = 128
IMG_DEV = 16
HALF = 3
IMAGES = 12288
PAIRS = 98304
N_OUTER = 32
N_INNER = 24


def centers(key):
    coarse = jax.random.normal(jax.random.fold_in(key, 101), (16, D), jnp.float32)
    fine_dirs = jax.random.normal(jax.random.fold_in(key, 102), (256, D), jnp.float32)
    return (coarse, fine_dirs)


def cluster_rows(key, row_count, coarse, fine_dirs):
    keys = jax.random.split(key, 5)
    coarse_pick = jax.random.randint(keys[0], (row_count,), 0, 16)
    fine_pick = jax.random.randint(keys[1], (row_count,), 0, 256)
    coarse_weight = jax.random.uniform(keys[2], (row_count, 1), jnp.float32, -1.2, 1.2)
    fine_weight = jax.random.uniform(keys[3], (row_count, 1), jnp.float32, -1.0, 1.0)
    gaussian = jax.random.normal(keys[4], (row_count, D), jnp.float32)
    mixed_noise = gaussian
    values = coarse_weight * jnp.take(coarse, coarse_pick, axis=0)
    values = values + fine_weight * jnp.take(fine_dirs, fine_pick, axis=0)
    return values + 0.6 * mixed_noise


def image_latent(key):
    coarse, fine_dirs = centers(key)
    return cluster_rows(jax.random.fold_in(key, 31), IMAGES, coarse, fine_dirs)


def draw_images(key, part):
    latent = image_latent(key)
    key = jax.random.fold_in(key, 11)
    scales = jnp.exp(jax.random.uniform(key, (IMAGES, 1), jnp.float32, math.log(0.5), math.log(5.0)))
    return (latent * scales * (1.0 / math.sqrt(D))).astype(jnp.bfloat16)


def draw_texts(key, part):
    paired = image_latent(key)
    coarse, fine_dirs = centers(key)
    key = jax.random.fold_in(key, 23)
    key_scale, key_rows, key_pair = jax.random.split(key, 3)
    scales = jnp.exp(jax.random.uniform(key_scale, (PAIRS, 1), jnp.float32, math.log(0.5), math.log(5.0)))
    own_rows = cluster_rows(key_rows, PAIRS, coarse, fine_dirs)
    blocks = PAIRS // TXT_DEV
    own_rows = own_rows.reshape(blocks, TXT_DEV, D)
    paired = paired.reshape(blocks, IMG_DEV, D)
    pair_weight = jax.random.uniform(key_pair, (blocks, IMG_DEV, 1), jnp.float32, 0.3, 0.9)
    paired_rows = pair_weight * paired + jnp.sqrt(1.0 - pair_weight * pair_weight) * own_rows[:, :IMG_DEV]
    values = jnp.concatenate([paired_rows, own_rows[:, IMG_DEV:]], axis=1).reshape(PAIRS, D)
    return (values * scales * (0.3 / math.sqrt(D))).astype(jnp.bfloat16)


def setup_inputs(seed: int = 0) -> dict:
    splits = jax.random.split(jax.random.key(seed), 5)
    return {
        "images": draw_images(jax.random.fold_in(splits[4], 71), 0),
        "texts": draw_texts(jax.random.fold_in(splits[4], 71), 0),
        "logit_scale": jnp.clip(jnp.exp(jax.random.uniform(splits[2], (1,), jnp.float32, math.log(8.0), math.log(20.0))), 8.0, 20.0),
        "logit_bias": jnp.clip(jax.random.uniform(splits[3], (1,), jnp.float32, -2.0, 0.0), -2.0, 0.0),
    }


def unit_rows(values):
    widened = values.astype(jnp.float32)
    inverse = lax.rsqrt(lax.optimization_barrier(jnp.sum(widened * widened, axis=-1, keepdims=True)) + 1e-06)
    return (inverse, widened * inverse)

def project_back(inverse, unit_full, gradient):
    along = lax.optimization_barrier(jnp.sum(unit_full * gradient, axis=-1, keepdims=True))
    return inverse * (gradient - unit_full * along)

def pair_weights(logits, labels, divisor):
    return (-labels * jax.nn.sigmoid(-labels * logits) * divisor).astype(jnp.bfloat16)

def reference(images, texts, logit_scale, logit_bias):
    n_outer = N_OUTER
    group_img = IMG_DEV * N_INNER
    group_txt = TXT_DEV * N_INNER
    width = 2 * HALF + 1
    divisor = 1.0 / math.sqrt(width * group_txt)
    factor = logit_scale[0]
    offset = logit_bias[0]
    inverse_img, full_img = unit_rows(images)
    inverse_txt, full_txt = unit_rows(texts)
    img_groups = full_img.astype(jnp.bfloat16).reshape(n_outer, group_img, D)
    txt_groups = full_txt.astype(jnp.bfloat16).reshape(n_outer, group_txt, D)
    offsets = jnp.arange(-HALF, HALF + 1, dtype=jnp.int32)

    def positive_text(img_index):
        return img_index // IMG_DEV * TXT_DEV + img_index % IMG_DEV

    def image_side(group):
        chosen = ((group + offsets) % n_outer).astype(jnp.int32)
        window = jnp.take(txt_groups, chosen, axis=0).reshape(width * group_txt, D)
        txt_index = (chosen[:, None] * group_txt + jnp.arange(group_txt, dtype=jnp.int32)[None, :]).reshape(-1)
        img_index = group * group_img + jnp.arange(group_img, dtype=jnp.int32)
        own_rows = jnp.take(img_groups, group, axis=0)
        logits = jnp.dot(own_rows, window.T, preferred_element_type=jnp.float32) * factor + offset
        labels = jnp.where(positive_text(img_index)[:, None] == txt_index[None, :], 1.0, -1.0).astype(jnp.float32)
        weights = pair_weights(logits, labels, divisor)
        return jnp.dot(weights, window, preferred_element_type=jnp.float32) * factor

    def text_side(group):
        chosen = ((group + offsets) % n_outer).astype(jnp.int32)
        window = jnp.take(img_groups, chosen, axis=0).reshape(width * group_img, D)
        img_index = (chosen[:, None] * group_img + jnp.arange(group_img, dtype=jnp.int32)[None, :]).reshape(-1)
        txt_index = group * group_txt + jnp.arange(group_txt, dtype=jnp.int32)
        own_rows = jnp.take(txt_groups, group, axis=0)
        logits = jnp.dot(window, own_rows.T, preferred_element_type=jnp.float32) * factor + offset
        labels = jnp.where(positive_text(img_index)[:, None] == txt_index[None, :], 1.0, -1.0).astype(jnp.float32)
        weights = pair_weights(logits, labels, divisor)
        return jnp.dot(weights.T, window, preferred_element_type=jnp.float32) * factor
    groups = jnp.arange(n_outer, dtype=jnp.int32)
    image_total = lax.map(image_side, groups).reshape(IMAGES, D)
    text_total = lax.map(text_side, groups).reshape(PAIRS, D)
    return (project_back(inverse_img, full_img, image_total), project_back(inverse_txt, full_txt, text_total))
```

```python
import functools
import math

import jax
import jax.numpy as jnp
from jax import lax
from jax.experimental import pallas as pl
from jax.experimental.pallas import tpu as pltpu
from jax.sharding import PartitionSpec as P

MESH = pl.DeviceIdType.MESH
HALF = 3
D = 1152
IMG = 16
TXT = 128
NO, NI = 32, 24
NZ = 12

STAGE_Z = ((0, 1, -1, 2, -2), (3, -3, 4, -4), (5, -5, 6))
STAGES = tuple(tuple((dz, dy) for dy in (0, 1) for dz in zs) for zs in STAGE_Z)
SLOTS = tuple(slot for stage in STAGES for slot in stage)
INDEX = {slot: n for n, slot in enumerate(SLOTS)}
STAGE_AT = (0, 10, 18, 24)
FAR_Z = (6, 5, -5, 4, -4)
Z_SLOTS = (1, -1, 2, -2, 3, -3, 4, -4, 5, -5, 6)
Z_INDEX = {dz: n for n, dz in enumerate(Z_SLOTS)}


def sign(value):
    return (value > 0) - (value < 0)


def gather_parent(slot):
    dz, dy = slot
    if dz == 0:
        return (0, 0)
    return (sign(dz) * ((abs(dz) - 1) // 2 * 2), dy)


KIDS = {
    slot: tuple(kid for kid in reversed(SLOTS) if kid != (0, 0) and gather_parent(kid) == slot)
    for slot in SLOTS
}


def unit_rows(values):
    widened = values.astype(jnp.float32)
    inverse = lax.rsqrt(jnp.sum(widened * widened, axis=-1, keepdims=True) + 1e-06)
    return inverse, widened * inverse


def project_back(inverse, unit_full, gradient):
    along = jnp.sum(unit_full * gradient, axis=-1, keepdims=True)
    return inverse * (gradient - unit_full * along)


def kernel(
    scale_ref, bias_ref, img_hbm, txt_hbm, gi_ref, gt_ref,
    img_in, txt_in, img, txt, img_acc, txt_acc,
    y_send, y_recv, z_send, z_recv, g_send, g_recv, p_recv,
    in_sem, ag_ss, ag_rs, t_ss, t_rs, y_ss, y_rs, z_ss, z_rs, g_ss, g_rs, p_ss, p_rs,
):
    o = lax.axis_index("outer")
    i = lax.axis_index("inner")
    core = o % 2
    x = (o // 2) % 4
    z = i // 2
    yl = i % 2
    divisor = 1.0 / math.sqrt((2 * HALF + 1) * NI * TXT)

    def along_z(dz, flip):
        return (o, ((z + dz + NZ) % NZ) * 2 + (1 - yl if flip else yl))

    last = (x // 3) * yl
    first = ((3 - x) // 3) * yl
    partner = (o + 1 - 2 * core, i)
    up = ((o + 2 - 8 * last + NO) % NO, i)
    down = ((o - 2 + 8 * first + NO) % NO, i)
    true_up = ((o + 2) % NO, i)
    true_down = ((o - 2 + NO) % NO, i)
    far = ((o - 1 + 2 * core + NO) % NO, i)
    up_row = ((o + 8) % NO, i)
    down_row = ((o - 8 + NO) % NO, i)

    barrier = pltpu.get_barrier_semaphore()

    def greet(device):
        pl.semaphore_signal(barrier, inc=1, device_id=device, device_id_type=MESH)

    peers = [along_z(0, True)] + [along_z(dz, False) for dz in (1, -1, 2, -2, 3, -3)]
    peers += [partner, far, true_up, true_down]
    for peer in peers:
        greet(peer)

    @pl.when(yl == 1)
    def _():
        @pl.when(x == 0)
        def _():
            greet(((o + 6) % NO, i))
            greet(up_row)
            greet(down_row)

        @pl.when(x == 3)
        def _():
            greet(((o - 6 + NO) % NO, i))
            greet(up_row)
            greet(down_row)

    load_img = pltpu.make_async_copy(img_hbm, img_in, in_sem.at[0])
    load_txt = pltpu.make_async_copy(txt_hbm, txt_in, in_sem.at[1])
    load_img.start()
    load_txt.start()
    load_img.wait()
    _, full = unit_rows(img_in[...])
    img[0:IMG, :] = full.astype(jnp.bfloat16)

    through = yl * (1 - ((x + 1) // 2) % 2)
    pl.semaphore_wait(barrier, len(peers) + 3 * through)

    def gather_copy(kid):
        dz, dy = kid
        pz, py = gather_parent(kid)
        a, b = INDEX[(pz, py)], INDEX[kid]
        return pltpu.make_async_remote_copy(
            src_ref=img.at[a * IMG:(a + 1) * IMG],
            dst_ref=img.at[b * IMG:(b + 1) * IMG],
            send_sem=ag_ss.at[b],
            recv_sem=ag_rs.at[b],
            device_id=along_z(dz - pz, dy != py),
            device_id_type=MESH,
        )

    def pass_on(slot):
        if slot != (0, 0):
            gather_copy(slot).wait_recv()
        for kid in KIDS[slot]:
            gather_copy(kid).start()

    def text_copy(source, slot, n, device):
        return pltpu.make_async_remote_copy(
            src_ref=txt.at[source],
            dst_ref=txt.at[slot],
            send_sem=t_ss.at[n],
            recv_sem=t_rs.at[slot],
            device_id=device,
            device_id_type=MESH,
        )

    text_partner = text_copy(0, 1, 1, partner)
    text_up = text_copy(0, 2 + 5 * last, 2, up)
    text_down = text_copy(0, 3 + 5 * first, 3, down)
    text_four = text_copy(2, 4, 4, partner)
    text_five = text_copy(3, 5, 5, partner)
    text_far = text_copy(3 - core, 6, 6, far)
    text_up_row = text_copy(7, 2, 7, up_row)
    text_down_row = text_copy(8, 3, 8, down_row)

    def text_arrived(slot):
        text_copy(0, slot, 0, partner).wait_recv()

    pass_on((0, 0))
    load_txt.wait()
    _, full = unit_rows(txt_in[...])
    txt[0] = full.astype(jnp.bfloat16)
    text_up.start()
    text_down.start()
    text_partner.start()
    pass_on((0, 1))

    factor = scale_ref[0]
    offset = bias_ref[0]

    def tile(stage, slots, first_rows, first_cols):
        r0, r1 = STAGE_AT[stage] * IMG, STAGE_AT[stage + 1] * IMG
        s0, n = slots[0], len(slots)
        rows = img[r0:r1, :]
        cols = txt[s0:s0 + n].reshape(n * TXT, D)
        logits = lax.dot_general(
            rows, cols, (((1,), (1,)), ((), ())), preferred_element_type=jnp.float32
        ) * factor + offset
        if stage == 0 and s0 == 0:
            shape = (r1 - r0, n * TXT)
            r = lax.broadcasted_iota(jnp.int32, shape, 0)
            c = lax.broadcasted_iota(jnp.int32, shape, 1)
            matched = jnp.logical_and(r == c, r < IMG)
            label = jnp.where(matched, 1.0, -1.0)
            weights = -label / (1.0 + jnp.exp(label * logits)) * divisor
        else:
            weights = divisor / (1.0 + jnp.exp(-logits))
        weights = weights.astype(jnp.bfloat16)
        image_part = jnp.dot(weights, cols, preferred_element_type=jnp.float32)
        text_part = lax.dot_general(
            weights, rows, (((0,), (0,)), ((), ())), preferred_element_type=jnp.float32
        ).reshape(n, TXT, D)
        if first_rows:
            img_acc[r0:r1, :] = image_part
        else:
            img_acc[r0:r1, :] += image_part
        if first_cols:
            txt_acc[s0:s0 + n] = text_part
        else:
            txt_acc[s0:s0 + n] += text_part

    pass_on((2, 0))
    pass_on((-2, 0))

    def relay(here, slot, onward):
        @pl.when(yl == 1)
        def _():
            @pl.when(x == here)
            def _():
                text_arrived(slot)
                onward.start()

    relay(0, 7, text_up_row)
    relay(3, 8, text_down_row)
    pass_on((2, 1))
    pass_on((-2, 1))
    for slot in ((1, 0), (-1, 0), (1, 1), (-1, 1)):
        pass_on(slot)
    text_arrived(1)
    tile(0, (0, 1), True, True)
    for slot in ((4, 0), (-4, 0), (4, 1), (-4, 1)):
        pass_on(slot)
    text_arrived(2)
    text_arrived(3)
    text_far.start()
    text_four.start()
    text_five.start()
    tile(0, (2, 3), False, True)
    for slot in ((3, 0), (-3, 0), (3, 1), (-3, 1)):
        pass_on(slot)
    tile(1, (0, 1), True, False)
    tile(1, (2, 3), False, False)
    text_arrived(4)
    text_arrived(5)
    tile(0, (4, 5), False, True)
    tile(1, (4, 5), False, False)
    text_arrived(6)
    tile(0, (6,), False, True)
    tile(1, (6,), False, False)
    for slot in STAGES[2]:
        pass_on(slot)

    def grad_copy(source, slot, n, device):
        return pltpu.make_async_remote_copy(
            src_ref=source,
            dst_ref=g_recv.at[slot],
            send_sem=g_ss.at[n],
            recv_sem=g_rs.at[slot],
            device_id=device,
            device_id_type=MESH,
        )

    def pair_copy(slot, n):
        return pltpu.make_async_remote_copy(
            src_ref=txt_acc.at[slot],
            dst_ref=p_recv.at[n],
            send_sem=p_ss.at[n],
            recv_sem=p_rs.at[n],
            device_id=partner,
            device_id_type=MESH,
        )

    grad_far = grad_copy(g_send.at[2], 2, 2, far)
    grad_up = grad_copy(g_send.at[1], 3 * last, 0, up)
    grad_down = grad_copy(g_send.at[0], 1 + 3 * first, 1, down)
    grad_up_row = grad_copy(g_recv.at[3], 0, 3, up_row)
    grad_down_row = grad_copy(g_recv.at[4], 1, 4, down_row)
    pair_own, pair_four, pair_five = pair_copy(1, 0), pair_copy(4, 1), pair_copy(5, 2)

    def grad_arrived(slot):
        grad_copy(g_send.at[0], slot, 0, partner).wait_recv()

    def y_copy(stage):
        a, b = STAGE_AT[stage] * IMG // 2, STAGE_AT[stage + 1] * IMG // 2
        return pltpu.make_async_remote_copy(
            src_ref=y_send.at[a:b],
            dst_ref=y_recv.at[a:b],
            send_sem=y_ss.at[stage],
            recv_sem=y_rs.at[stage],
            device_id=along_z(0, True),
            device_id_type=MESH,
        )

    def y_start(stage):
        a, b = STAGE_AT[stage] * IMG // 2, STAGE_AT[stage + 1] * IMG // 2
        y_send[a:b, :] = img_acc[a + b:2 * b, :].astype(jnp.bfloat16)
        y_copy(stage).start()

    def z_copy(dz):
        n = Z_INDEX[dz]
        hop = dz - sign(dz) * 3 if abs(dz) > 3 else dz
        return pltpu.make_async_remote_copy(
            src_ref=z_send.at[n],
            dst_ref=z_recv.at[n],
            send_sem=z_ss.at[n],
            recv_sem=z_rs.at[n],
            device_id=along_z(-hop, False),
            device_id_type=MESH,
        )

    def y_sum(dz):
        stage = 0 if abs(dz) < 3 else 1 if abs(dz) < 5 else 2
        a = INDEX[(dz, 0)] * IMG
        b = STAGE_AT[stage] * IMG // 2 + STAGE_Z[stage].index(dz) * IMG
        return img_acc[a:a + IMG, :] + y_recv[b:b + IMG, :].astype(jnp.float32)

    def z_start(dz, total):
        z_send[Z_INDEX[dz]] = total.astype(jnp.bfloat16)
        z_copy(dz).start()

    def z_got(dz):
        z_copy(dz).wait_recv()
        return z_recv[Z_INDEX[dz]].astype(jnp.float32)

    tile(2, (6,), True, False)
    g_send[2] = txt_acc[6].astype(jnp.bfloat16)
    grad_far.start()
    tile(2, (4, 5), False, False)
    pair_four.start()
    pair_five.start()
    tile(2, (2, 3), False, False)
    tile(2, (0, 1), False, False)
    y_start(2)
    y_start(1)
    y_start(0)
    pair_own.start()

    pair_four.wait_recv()
    g_send[0] = (txt_acc[2] + p_recv[1]).astype(jnp.bfloat16)
    pair_five.wait_recv()
    g_send[1] = (txt_acc[3] + p_recv[2]).astype(jnp.bfloat16)
    grad_arrived(2)

    @pl.when(core == 1)
    def _():
        g_send[0] = (txt_acc[2] + p_recv[1] + g_recv[2].astype(jnp.float32)).astype(jnp.bfloat16)

    @pl.when(core == 0)
    def _():
        g_send[1] = (txt_acc[3] + p_recv[2] + g_recv[2].astype(jnp.float32)).astype(jnp.bfloat16)

    grad_down.start()
    grad_up.start()

    y_copy(2).wait_recv()
    for dz in (6, 5, -5):
        z_start(dz, y_sum(dz))
    y_copy(1).wait_recv()
    for dz in (4, -4):
        z_start(dz, y_sum(dz))
    y_copy(0).wait_recv()
    for dz in (2, -2, 1, -1):
        z_start(dz, y_sum(dz))

    @pl.when(yl == 1)
    def _():
        @pl.when(x == 0)
        def _():
            grad_arrived(3)
            grad_up_row.start()

        @pl.when(x == 3)
        def _():
            grad_arrived(4)
            grad_down_row.start()

    z_start(3, y_sum(3) + z_got(4) + z_got(5) + z_got(6))
    z_start(-3, y_sum(-3) + z_got(-4) + z_got(-5))

    pair_own.wait_recv()
    text_total = txt_acc[0] + p_recv[0]
    grad_arrived(0)
    grad_arrived(1)
    text_total = text_total + (g_recv[0].astype(jnp.float32) + g_recv[1].astype(jnp.float32))
    inverse, full = unit_rows(txt_in[...])
    gt_ref[...] = project_back(inverse, full, text_total * factor)

    image_total = y_sum(0)
    for dz in (1, -1, 2, -2, 3, -3):
        image_total = image_total + z_got(dz)
    inverse, full = unit_rows(img_in[...])
    gi_ref[...] = project_back(inverse, full, image_total * factor)

    for slot in SLOTS[1:]:
        gather_copy(slot).wait_send()
    for copy in (
        text_partner, text_up, text_down, text_four, text_five, text_far,
        grad_far, grad_up, grad_down, pair_own, pair_four, pair_five,
        y_copy(0), y_copy(1), y_copy(2),
    ):
        copy.wait_send()
    for dz in Z_SLOTS:
        z_copy(dz).wait_send()

    @pl.when(yl == 1)
    def _():
        @pl.when(x == 0)
        def _():
            text_up_row.wait_send()
            grad_up_row.wait_send()

        @pl.when(x == 3)
        def _():
            text_down_row.wait_send()
            grad_down_row.wait_send()


def local(images, texts, logit_scale, logit_bias):
    bf, f32 = jnp.bfloat16, jnp.float32
    dma = pltpu.SemaphoreType.DMA
    return pl.pallas_call(
        kernel,
        out_shape=(
            jax.ShapeDtypeStruct((IMG, D), f32),
            jax.ShapeDtypeStruct((TXT, D), f32),
        ),
        in_specs=[pl.BlockSpec(memory_space=pltpu.SMEM)] * 2
        + [pl.BlockSpec(memory_space=pl.ANY)] * 2,
        out_specs=[pl.BlockSpec(memory_space=pltpu.VMEM)] * 2,
        scratch_shapes=[
            pltpu.VMEM((IMG, D), bf),
            pltpu.VMEM((TXT, D), bf),
            pltpu.VMEM((NI * IMG, D), bf),
            pltpu.VMEM((9, TXT, D), bf),
            pltpu.VMEM((NI * IMG, D), f32),
            pltpu.VMEM((7, TXT, D), f32),
            pltpu.VMEM((NI * IMG // 2, D), bf),
            pltpu.VMEM((NI * IMG // 2, D), bf),
            pltpu.VMEM((11, IMG, D), bf),
            pltpu.VMEM((11, IMG, D), bf),
            pltpu.VMEM((3, TXT, D), bf),
            pltpu.VMEM((5, TXT, D), bf),
            pltpu.VMEM((3, TXT, D), f32),
            dma((2,)),
            dma((NI,)), dma((NI,)),
            dma((9,)), dma((9,)),
            dma((3,)), dma((3,)),
            dma((11,)), dma((11,)),
            dma((5,)), dma((5,)),
            dma((3,)), dma((3,)),
        ],
        compiler_params=pltpu.CompilerParams(
            collective_id=0, has_side_effects=True, vmem_limit_bytes=48 << 20
        ),
        name="pair_gradients",
    )(logit_scale, logit_bias, images, texts)


def solution(mesh):
    return jax.shard_map(
        local,
        mesh=mesh,
        in_specs=(P(("outer", "inner"), None), P(("outer", "inner"), None), P(), P()),
        out_specs=(P(("outer", "inner"), None), P(("outer", "inner"), None)),
        check_vma=False,
    )
```

```python
import functools
import math

import jax
import jax.numpy as jnp
from jax import lax
from jax.experimental import pallas as pl
from jax.experimental.pallas import tpu as pltpu
from jax.sharding import PartitionSpec as P

MESH = pl.DeviceIdType.MESH
HALF = 3
D = 1152
IMG = 16
TXT = 128
NO, NI = 32, 24
NZ = 12

STAGE_Z = ((0, 1, -1, 2, -2), (3, -3, 4, -4), (5, -5, 6))
STAGES = tuple(tuple((dz, dy) for dy in (0, 1) for dz in zs) for zs in STAGE_Z)
SLOTS = tuple(slot for stage in STAGES for slot in stage)
INDEX = {slot: n for n, slot in enumerate(SLOTS)}
STAGE_AT = (0, 10, 18, 24)
PARTS = 4
PART = TXT // PARTS
Z_SLOTS = (1, -1, 2, -2, 3, -3, 4, -4, 5, -5, 6)
Z_INDEX = {dz: n for n, dz in enumerate(Z_SLOTS)}


def sign(value):
    return (value > 0) - (value < 0)


def gather_parent(slot):
    dz, dy = slot
    if dz == 0:
        return (0, 0)
    return (sign(dz) * ((abs(dz) - 1) // 2 * 2), dy)


KIDS = {
    slot: tuple(kid for kid in reversed(SLOTS) if kid != (0, 0) and gather_parent(kid) == slot)
    for slot in SLOTS
}


def unit_rows(values):
    widened = values.astype(jnp.float32)
    inverse = lax.rsqrt(jnp.sum(widened * widened, axis=-1, keepdims=True) + 1e-06)
    return inverse, widened * inverse


def project_back(inverse, unit_full, gradient):
    along = jnp.sum(unit_full * gradient, axis=-1, keepdims=True)
    return inverse * (gradient - unit_full * along)


def kernel(
    scale_hbm, bias_hbm, img_hbm, txt_hbm, gi_ref, gt_ref,
    scale, bias, img_in, txt_in, img, txt, img_acc, txt_acc,
    y_send, y_recv, z_send, z_recv, g_send, g_recv, p_recv,
    in_sem, ag_ss, ag_rs, t_ss, t_rs, y_ss, y_rs, z_ss, z_rs, g_ss, g_rs, p_ss, p_rs,
):
    o = lax.axis_index("outer")
    i = lax.axis_index("inner")
    core = o % 2
    x = (o // 2) % 4
    z = i // 2
    yl = i % 2
    divisor = 1.0 / math.sqrt((2 * HALF + 1) * NI * TXT)

    def along_z(dz, flip):
        return (o, ((z + dz + NZ) % NZ) * 2 + (1 - yl if flip else yl))

    def at(shift):
        return ((o + shift + NO) % NO, i)

    last_x = x // 3
    first_x = (3 - x) // 3
    last = last_x * yl
    first = first_x * yl
    through = last + first
    inner_end = last_x * core + first_x * (1 - core)
    outer_end = (x // 2) * (1 - x % 2) * core + (x % 2) * (1 - x // 2) * (1 - core)
    side = 2 * core - 1

    barrier = pltpu.get_barrier_semaphore()

    def greet(device):
        pl.semaphore_signal(barrier, inc=1, device_id=device, device_id_type=MESH)

    peers = [along_z(0, True)] + [along_z(dz, False) for dz in (1, -1, 2, -2, 3, -3)]
    peers += [at(1 - 2 * core), at(side), at(2), at(-2)]
    for peer in peers:
        greet(peer)

    @pl.when(through == 1)
    def _():
        greet(at(6 * first_x - 6 * last_x))
        greet(at(8))
        greet(at(-8))

    @pl.when(inner_end == 1)
    def _():
        greet(at(3 * side))
        greet(at(-5 * side))

    @pl.when(outer_end == 1)
    def _():
        greet(at(3 * side))
        greet(at(-5 * side))
        greet(at(8))
        greet(at(-8))

    loads = [
        pltpu.make_async_copy(source, target, in_sem.at[n])
        for n, (source, target) in enumerate(
            ((img_hbm, img_in), (txt_hbm, txt_in), (scale_hbm, scale), (bias_hbm, bias))
        )
    ]
    for load in loads:
        load.start()
    loads[0].wait()
    _, full = unit_rows(img_in[...])
    img[0:IMG, :] = full.astype(jnp.bfloat16)

    pl.semaphore_wait(barrier, len(peers) + 3 * through + 2 * inner_end + 4 * outer_end)

    def gather_copy(kid):
        dz, dy = kid
        pz, py = gather_parent(kid)
        a, b = INDEX[(pz, py)], INDEX[kid]
        return pltpu.make_async_remote_copy(
            src_ref=img.at[a * IMG:(a + 1) * IMG],
            dst_ref=img.at[b * IMG:(b + 1) * IMG],
            send_sem=ag_ss.at[b],
            recv_sem=ag_rs.at[b],
            device_id=along_z(dz - pz, dy != py),
            device_id_type=MESH,
        )

    def pass_on(slot):
        if slot != (0, 0):
            gather_copy(slot).wait_recv()
        for kid in KIDS[slot]:
            gather_copy(kid).start()

    def text_copy(source, slot, n, device, part):
        rows = pl.ds(part * PART, PART)
        return pltpu.make_async_remote_copy(
            src_ref=txt.at[source, rows],
            dst_ref=txt.at[slot, rows],
            send_sem=t_ss.at[n, part],
            recv_sem=t_rs.at[slot, part],
            device_id=device,
            device_id_type=MESH,
        )

    def text_copies(source, slot, n, device):
        return [text_copy(source, slot, n, device, part) for part in range(PARTS)]

    partner = at(1 - 2 * core)
    up = at(2 - 8 * last)
    down = at(8 * first - 2)
    text_partner = text_copies(0, 1, 1, partner)
    text_up = text_copies(0, 2 + 5 * last, 2, up)
    text_down = text_copies(0, 3 + 5 * first, 3, down)
    text_four = text_copies(2, 4, 4, partner)
    text_five = text_copies(3, 5, 5, partner)
    text_far = text_copies(3 - core, 6, 6, at(side))
    text_far_own = text_copies(0, 6, 0, at(3 * side))
    text_through = text_copies(7 + last, 2 + last, 7, at(8 * first - 8 * last))

    def text_arrived(slot, part):
        text_copy(0, slot, 0, partner, part).wait_recv()

    def all_arrived(slot):
        for part in range(PARTS):
            text_arrived(slot, part)

    pass_on((0, 0))
    loads[1].wait()
    _, full = unit_rows(txt_in[...])
    txt[0] = full.astype(jnp.bfloat16)
    for part in range(PARTS):
        text_up[part].start()
        text_down[part].start()

    @pl.when(outer_end == 1)
    def _():
        for part in range(PARTS):
            text_far_own[part].start()

    for part in range(PARTS):
        text_partner[part].start()
    pass_on((0, 1))
    loads[2].wait()
    loads[3].wait()
    factor = scale[0]
    offset = bias[0]

    def tile(first_stage, last_stage, slots, first_rows, first_cols):
        r0, r1 = STAGE_AT[first_stage] * IMG, STAGE_AT[last_stage + 1] * IMG
        s0, n = slots[0], len(slots)
        rows = img[r0:r1, :]
        cols = txt[s0:s0 + n].reshape(n * TXT, D)
        logits = lax.dot_general(
            cols, rows, (((1,), (1,)), ((), ())), preferred_element_type=jnp.float32
        ) * factor + offset
        if r0 == 0 and s0 == 0:
            shape = (n * TXT, r1 - r0)
            t = lax.broadcasted_iota(jnp.int32, shape, 0)
            r = lax.broadcasted_iota(jnp.int32, shape, 1)
            matched = jnp.logical_and(r == t, r < IMG)
            label = jnp.where(matched, 1.0, -1.0)
            weights = -label / (1.0 + jnp.exp(label * logits)) * divisor
        else:
            weights = divisor / (1.0 + jnp.exp(-logits))
        weights = weights.astype(jnp.bfloat16)
        text_part = jnp.dot(weights, rows, preferred_element_type=jnp.float32).reshape(n, TXT, D)
        image_part = lax.dot_general(
            weights, cols, (((0,), (0,)), ((), ())), preferred_element_type=jnp.float32
        )
        if first_rows:
            img_acc[r0:r1, :] = image_part
        else:
            img_acc[r0:r1, :] += image_part
        if first_cols:
            txt_acc[s0:s0 + n] = text_part
        else:
            txt_acc[s0:s0 + n] += text_part

    def y_copy(stage):
        a, b = STAGE_AT[stage] * IMG // 2, STAGE_AT[stage + 1] * IMG // 2
        return pltpu.make_async_remote_copy(
            src_ref=y_send.at[a:b],
            dst_ref=y_recv.at[a:b],
            send_sem=y_ss.at[stage],
            recv_sem=y_rs.at[stage],
            device_id=along_z(0, True),
            device_id_type=MESH,
        )

    def y_start(stage):
        a, b = STAGE_AT[stage] * IMG // 2, STAGE_AT[stage + 1] * IMG // 2
        y_send[a:b, :] = img_acc[a + b:2 * b, :].astype(jnp.bfloat16)
        y_copy(stage).start()

    for slot in ((2, 0), (-2, 0), (2, 1), (-2, 1)):
        pass_on(slot)
    for slot in ((1, 0), (-1, 0), (1, 1), (-1, 1)):
        pass_on(slot)
    all_arrived(1)
    tile(0, 0, (0, 1), True, True)

    @pl.when(through == 1)
    def _():
        for part in range(PARTS):
            text_arrived(7 + last, part)
            text_through[part].start()

    for slot in ((4, 0), (-4, 0), (4, 1), (-4, 1)):
        pass_on(slot)
    for part in range(PARTS):
        text_arrived(2, part)
        text_arrived(3, part)

        @pl.when(inner_end == 0)
        def _():
            text_far[part].start()

        text_four[part].start()
        text_five[part].start()
    tile(0, 0, (2, 3), False, True)
    for slot in ((3, 0), (-3, 0), (3, 1), (-3, 1)):
        pass_on(slot)
    tile(1, 1, (0, 1, 2, 3), True, False)
    all_arrived(4)
    all_arrived(5)
    tile(0, 1, (4, 5), False, True)
    all_arrived(6)
    tile(0, 1, (6,), False, True)
    y_start(1)
    y_start(0)
    for slot in STAGES[2]:
        pass_on(slot)

    def grad_copy(source, slot, n, device, part):
        return pltpu.make_async_remote_copy(
            src_ref=source.at[pl.ds(part * PART, PART)],
            dst_ref=g_recv.at[slot, pl.ds(part * PART, PART)],
            send_sem=g_ss.at[n, part],
            recv_sem=g_rs.at[slot, part],
            device_id=device,
            device_id_type=MESH,
        )

    def grad_copies(source, slot, n, device):
        return [grad_copy(source, slot, n, device, part) for part in range(PARTS)]

    def pair_copy(slot, n):
        return pltpu.make_async_remote_copy(
            src_ref=txt_acc.at[slot],
            dst_ref=p_recv.at[n],
            send_sem=p_ss.at[n],
            recv_sem=p_rs.at[n],
            device_id=partner,
            device_id_type=MESH,
        )

    far_shift = side * (1 - inner_end) - 5 * side * inner_end
    early_shift = core * (2 - 8 * last) + (1 - core) * (8 * first - 2)
    late_shift = (1 - core) * (2 - 8 * last) + core * (8 * first - 2)
    early_slot = core * 3 * last + (1 - core) * (1 + 3 * first)
    late_slot = (1 - core) * 3 * last + core * (1 + 3 * first)
    grad_far = grad_copies(g_send.at[2], 2 + 4 * inner_end, 2, at(far_shift))
    grad_early = grad_copies(g_send.at[0], early_slot, 0, at(early_shift))
    grad_late = grad_copies(g_send.at[1], late_slot, 1, at(late_shift))
    grad_through = grad_copies(g_recv.at[3 + last], last, 3, at(8 * first - 8 * last))
    grad_far_through = grad_copies(g_recv.at[6], 5, 4, at(-8 * side))
    pair_own, pair_early, pair_late = pair_copy(1, 0), pair_copy(5 - core, 2 - core), pair_copy(4 + core, 1 + core)

    def grad_arrived(slot, part):
        grad_copy(g_send.at[0], slot, 0, partner, part).wait_recv()

    def pair_arrived(n):
        pair_copy(1, n).wait_recv()

    def z_copy(dz):
        n = Z_INDEX[dz]
        hop = dz - sign(dz) * 3 if abs(dz) > 3 else dz
        return pltpu.make_async_remote_copy(
            src_ref=z_send.at[n],
            dst_ref=z_recv.at[n],
            send_sem=z_ss.at[n],
            recv_sem=z_rs.at[n],
            device_id=along_z(-hop, False),
            device_id_type=MESH,
        )

    def y_sum(dz):
        stage = 0 if abs(dz) < 3 else 1 if abs(dz) < 5 else 2
        a = INDEX[(dz, 0)] * IMG
        b = STAGE_AT[stage] * IMG // 2 + STAGE_Z[stage].index(dz) * IMG
        return img_acc[a:a + IMG, :] + y_recv[b:b + IMG, :].astype(jnp.float32)

    def z_start(dz, total):
        z_send[Z_INDEX[dz]] = total.astype(jnp.bfloat16)
        z_copy(dz).start()

    def z_got(dz):
        z_copy(dz).wait_recv()
        return z_recv[Z_INDEX[dz]].astype(jnp.float32)

    tile(2, 2, (4, 5, 6), True, False)
    pair_early.start()
    g_send[2] = txt_acc[6].astype(jnp.bfloat16)
    for copy in grad_far:
        copy.start()
    pair_late.start()
    tile(2, 2, (0, 1, 2, 3), False, False)
    y_start(2)
    pair_arrived(1 + core)
    for part in range(PARTS):
        rows = pl.ds(part * PART, PART)
        g_send[0, rows] = (txt_acc[2 + core, rows] + p_recv[1 + core, rows]).astype(jnp.bfloat16)
        grad_early[part].start()
    pair_own.start()

    y_copy(1).wait_recv()
    for dz in (4, -4):
        z_start(dz, y_sum(dz))
    y_copy(0).wait_recv()
    for dz in (2, -2, 1, -1):
        z_start(dz, y_sum(dz))
    y_copy(2).wait_recv()
    for dz in (6, 5, -5):
        z_start(dz, y_sum(dz))

    pair_arrived(2 - core)
    for part in range(PARTS):
        rows = pl.ds(part * PART, PART)

        @pl.when(inner_end == 0)
        def _():
            grad_arrived(2, part)
            g_send[1, rows] = (
                txt_acc[3 - core, rows] + p_recv[2 - core, rows] + g_recv[2, rows].astype(jnp.float32)
            ).astype(jnp.bfloat16)

        @pl.when(inner_end == 1)
        def _():
            g_send[1, rows] = (txt_acc[3 - core, rows] + p_recv[2 - core, rows]).astype(jnp.bfloat16)

        grad_late[part].start()

    @pl.when(outer_end == 1)
    def _():
        for part in range(PARTS):
            grad_arrived(6, part)
            grad_far_through[part].start()

    def go_through():
        for part in range(PARTS):
            grad_arrived(3 + last, part)
            grad_through[part].start()

    early_through = first * core + last * (1 - core)
    late_through = first * (1 - core) + last * core

    @pl.when(early_through == 1)
    def _():
        go_through()

    z_start(3, y_sum(3) + z_got(4) + z_got(5) + z_got(6))
    z_start(-3, y_sum(-3) + z_got(-4) + z_got(-5))

    @pl.when(late_through == 1)
    def _():
        go_through()

    inverse, full = unit_rows(img_in[...])
    image_total = y_sum(0)
    for dz in (1, -1, 2, -2, 3, -3):
        image_total = image_total + z_got(dz)
    gi_ref[...] = project_back(inverse, full, image_total * factor)

    pair_arrived(0)
    for part in range(PARTS):
        rows = pl.ds(part * PART, PART)
        grad_arrived(0, part)
        grad_arrived(1, part)
        txt_acc[0, rows] += p_recv[0, rows] + (
            g_recv[0, rows].astype(jnp.float32) + g_recv[1, rows].astype(jnp.float32)
        )

        @pl.when(outer_end == 1)
        def _():
            grad_arrived(5, part)
            txt_acc[0, rows] += g_recv[5, rows].astype(jnp.float32)

        inverse, full = unit_rows(txt_in[rows, :])
        gt_ref[rows, :] = project_back(inverse, full, txt_acc[0, rows] * factor)

    for slot in SLOTS[1:]:
        gather_copy(slot).wait_send()
    for dz in Z_SLOTS:
        z_copy(dz).wait_send()
    for copy in (y_copy(0), y_copy(1), y_copy(2), pair_own, pair_early, pair_late):
        copy.wait_send()
    for copies in (text_partner, text_up, text_down, text_four, text_five, grad_far, grad_early, grad_late):
        for copy in copies:
            copy.wait_send()

    @pl.when(inner_end == 0)
    def _():
        for copy in text_far:
            copy.wait_send()

    @pl.when(outer_end == 1)
    def _():
        for copy in text_far_own + grad_far_through:
            copy.wait_send()

    @pl.when(through == 1)
    def _():
        for copy in text_through + grad_through:
            copy.wait_send()


def local(images, texts, logit_scale, logit_bias):
    bf, f32 = jnp.bfloat16, jnp.float32
    dma = pltpu.SemaphoreType.DMA
    return pl.pallas_call(
        kernel,
        out_shape=(
            jax.ShapeDtypeStruct((IMG, D), f32),
            jax.ShapeDtypeStruct((TXT, D), f32),
        ),
        in_specs=[pl.BlockSpec(memory_space=pl.ANY)] * 4,
        out_specs=[pl.BlockSpec(memory_space=pltpu.VMEM)] * 2,
        scratch_shapes=[
            pltpu.SMEM((1,), f32),
            pltpu.SMEM((1,), f32),
            pltpu.VMEM((IMG, D), bf),
            pltpu.VMEM((TXT, D), bf),
            pltpu.VMEM((NI * IMG, D), bf),
            pltpu.VMEM((9, TXT, D), bf),
            pltpu.VMEM((NI * IMG, D), f32),
            pltpu.VMEM((7, TXT, D), f32),
            pltpu.VMEM((NI * IMG // 2, D), bf),
            pltpu.VMEM((NI * IMG // 2, D), bf),
            pltpu.VMEM((11, IMG, D), bf),
            pltpu.VMEM((11, IMG, D), bf),
            pltpu.VMEM((3, TXT, D), bf),
            pltpu.VMEM((7, TXT, D), bf),
            pltpu.VMEM((3, TXT, D), f32),
            dma((4,)),
            dma((NI,)), dma((NI,)),
            dma((8, PARTS)), dma((9, PARTS)),
            dma((3,)), dma((3,)),
            dma((11,)), dma((11,)),
            dma((5, PARTS)), dma((7, PARTS)),
            dma((3,)), dma((3,)),
        ],
        compiler_params=pltpu.CompilerParams(
            collective_id=0, has_side_effects=True, vmem_limit_bytes=48 << 20
        ),
        name="pair_gradients",
    )(logit_scale, logit_bias, images, texts)


def solution(mesh):
    return jax.shard_map(
        local,
        mesh=mesh,
        in_specs=(P(("outer", "inner"), None), P(("outer", "inner"), None), P(), P()),
        out_specs=(P(("outer", "inner"), None), P(("outer", "inner"), None)),
        check_vma=False,
    )
```

```python
import functools
import math

import jax
import jax.numpy as jnp
from jax import lax
from jax.experimental import pallas as pl
from jax.experimental.pallas import tpu as pltpu
from jax.sharding import PartitionSpec as P

MESH = pl.DeviceIdType.MESH
HALF = 3
D = 1152
IMG = 16
TXT = 128
NO, NI = 32, 24
NZ = 12

STAGE_Z = ((0, 1, -1, 2, -2), (3, -3, 4, -4), (5, -5, 6))
STAGES = tuple(tuple((dz, dy) for dy in (0, 1) for dz in zs) for zs in STAGE_Z)
SLOTS = tuple(slot for stage in STAGES for slot in stage)
INDEX = {slot: n for n, slot in enumerate(SLOTS)}
STAGE_AT = (0, 10, 18, 24)
PARTS = 4
PART = TXT // PARTS


def sign(value):
    return (value > 0) - (value < 0)


def tree_parent(slot):
    dz, dy = slot
    if dz == 6:
        return (4, 0) if dy == 0 else (-4, 1)
    if dz == 0:
        return (0, 0)
    if dz % 2 == 0:
        return (dz - 2 * sign(dz), dy)
    return (dz, 0) if dy else (dz - sign(dz), 0)


KIDS = {
    slot: tuple(
        sorted(
            (kid for kid in SLOTS if kid != (0, 0) and tree_parent(kid) == slot),
            key=lambda kid: (kid[1] == slot[1], kid[0] % 2, abs(kid[0])),
        )
    )
    for slot in SLOTS
}


def unit_rows(values):
    widened = values.astype(jnp.float32)
    inverse = lax.rsqrt(jnp.sum(widened * widened, axis=-1, keepdims=True) + 1e-06)
    return inverse, widened * inverse


def project_back(inverse, unit_full, gradient):
    along = jnp.sum(unit_full * gradient, axis=-1, keepdims=True)
    return inverse * (gradient - unit_full * along)


def kernel(
    scale_hbm, bias_hbm, img_hbm, txt_hbm, gi_hbm, gt_hbm,
    scale, bias, img_in, txt_in, img, txt, img_acc, txt_acc,
    i_send, i_recv, g_send, g_recv, p_recv, gi, gt,
    in_sem, out_sem, ag_ss, ag_rs, t_ss, t_rs, i_ss, i_rs, g_ss, g_rs, p_ss, p_rs,
):
    o = lax.axis_index("outer")
    i = lax.axis_index("inner")
    core = o % 2
    x = (o // 2) % 4
    z = i // 2
    yl = i % 2
    divisor = 1.0 / math.sqrt((2 * HALF + 1) * NI * TXT)

    def along_z(dz, flip):
        return (o, ((z + dz + NZ) % NZ) * 2 + (1 - yl if flip else yl))

    def at(shift):
        return ((o + shift + NO) % NO, i)

    last_x = x // 3
    first_x = (3 - x) // 3
    last = last_x * yl
    first = first_x * yl
    through = last + first
    inner_end = last_x * core + first_x * (1 - core)
    outer_end = (x // 2) * (1 - x % 2) * core + (x % 2) * (1 - x // 2) * (1 - core)
    side = 2 * core - 1

    barrier = pltpu.get_barrier_semaphore()

    def greet(device):
        pl.semaphore_signal(barrier, inc=1, device_id=device, device_id_type=MESH)

    peers = [along_z(0, True)] + [along_z(dz, False) for dz in (1, -1, 2, -2)]
    peers += [at(1 - 2 * core), at(side), at(2), at(-2)]
    for peer in peers:
        greet(peer)

    @pl.when(through == 1)
    def _():
        greet(at(6 * first_x - 6 * last_x))
        greet(at(8))
        greet(at(-8))

    @pl.when(inner_end == 1)
    def _():
        greet(at(3 * side))
        greet(at(-5 * side))

    @pl.when(outer_end == 1)
    def _():
        greet(at(3 * side))
        greet(at(-5 * side))
        greet(at(8))
        greet(at(-8))

    loads = [
        pltpu.make_async_copy(source, target, in_sem.at[n])
        for n, (source, target) in enumerate(
            ((img_hbm, img_in), (txt_hbm, txt_in), (scale_hbm, scale), (bias_hbm, bias))
        )
    ]
    for load in loads:
        load.start()
    loads[0].wait()
    _, full = unit_rows(img_in[...])
    img[0:IMG, :] = full.astype(jnp.bfloat16)

    pl.semaphore_wait(barrier, len(peers) + 3 * through + 2 * inner_end + 4 * outer_end)

    def gather_copy(kid):
        dz, dy = kid
        pz, py = tree_parent(kid)
        a, b = INDEX[(pz, py)], INDEX[kid]
        return pltpu.make_async_remote_copy(
            src_ref=img.at[a * IMG:(a + 1) * IMG],
            dst_ref=img.at[b * IMG:(b + 1) * IMG],
            send_sem=ag_ss.at[b],
            recv_sem=ag_rs.at[b],
            device_id=along_z(dz - pz, dy != py),
            device_id_type=MESH,
        )

    def pass_on(slot):
        if slot != (0, 0):
            gather_copy(slot).wait_recv()
        for kid in KIDS[slot]:
            gather_copy(kid).start()

    def text_copy(source, slot, n, device, part):
        rows = pl.ds(part * PART, PART)
        return pltpu.make_async_remote_copy(
            src_ref=txt.at[source, rows],
            dst_ref=txt.at[slot, rows],
            send_sem=t_ss.at[n, part],
            recv_sem=t_rs.at[slot, part],
            device_id=device,
            device_id_type=MESH,
        )

    def text_copies(source, slot, n, device):
        return [text_copy(source, slot, n, device, part) for part in range(PARTS)]

    partner = at(1 - 2 * core)
    up = at(2 - 8 * last)
    down = at(8 * first - 2)
    text_partner = text_copies(0, 1, 1, partner)
    text_up = text_copies(0, 2 + 5 * last, 2, up)
    text_down = text_copies(0, 3 + 5 * first, 3, down)
    text_four = text_copies(2, 4, 4, partner)
    text_five = text_copies(3, 5, 5, partner)
    text_far = text_copies(3 - core, 6, 6, at(side))
    text_far_own = text_copies(0, 6, 0, at(3 * side))
    text_through = text_copies(7 + last, 2 + last, 7, at(8 * first - 8 * last))

    def text_arrived(slot, part):
        text_copy(0, slot, 0, partner, part).wait_recv()

    def all_arrived(slot):
        for part in range(PARTS):
            text_arrived(slot, part)

    pass_on((0, 0))
    loads[1].wait()
    _, full = unit_rows(txt_in[...])
    txt[0] = full.astype(jnp.bfloat16)
    for part in range(PARTS):
        text_up[part].start()
        text_down[part].start()

    @pl.when(outer_end == 1)
    def _():
        for part in range(PARTS):
            text_far_own[part].start()

    for part in range(PARTS):
        text_partner[part].start()
    pass_on((0, 1))
    loads[2].wait()
    loads[3].wait()
    factor = scale[0]
    offset = bias[0]

    def tile(first_stage, last_stage, slots, first_rows, first_cols):
        r0, r1 = STAGE_AT[first_stage] * IMG, STAGE_AT[last_stage + 1] * IMG
        s0, n = slots[0], len(slots)
        rows = img[r0:r1, :]
        cols = txt[s0:s0 + n].reshape(n * TXT, D)
        logits = lax.dot_general(
            cols, rows, (((1,), (1,)), ((), ())), preferred_element_type=jnp.float32
        ) * factor + offset
        if r0 == 0 and s0 == 0:
            shape = (n * TXT, r1 - r0)
            t = lax.broadcasted_iota(jnp.int32, shape, 0)
            r = lax.broadcasted_iota(jnp.int32, shape, 1)
            matched = jnp.logical_and(r == t, r < IMG)
            label = jnp.where(matched, 1.0, -1.0)
            weights = -label / (1.0 + jnp.exp(label * logits)) * divisor
        else:
            weights = divisor / (1.0 + jnp.exp(-logits))
        weights = weights.astype(jnp.bfloat16)
        text_part = jnp.dot(weights, rows, preferred_element_type=jnp.float32).reshape(n, TXT, D)
        image_part = lax.dot_general(
            weights, cols, (((0,), (0,)), ((), ())), preferred_element_type=jnp.float32
        )
        if first_rows:
            img_acc[r0:r1, :] = image_part
        else:
            img_acc[r0:r1, :] += image_part
        if first_cols:
            txt_acc[s0:s0 + n] = text_part
        else:
            txt_acc[s0:s0 + n] += text_part

    for slot in ((2, 0), (-2, 0), (2, 1), (-2, 1), (1, 0), (-1, 0), (1, 1), (-1, 1)):
        pass_on(slot)
    all_arrived(1)
    tile(0, 0, (0, 1), True, True)

    @pl.when(through == 1)
    def _():
        for part in range(PARTS):
            text_arrived(7 + last, part)
            text_through[part].start()

    for slot in ((4, 0), (-4, 0), (4, 1), (-4, 1)):
        pass_on(slot)
    for part in range(PARTS):
        text_arrived(2, part)
        text_arrived(3, part)

        @pl.when(inner_end == 0)
        def _():
            text_far[part].start()

        text_four[part].start()
        text_five[part].start()
    pass_on((3, 0))
    pass_on((-3, 0))
    tile(0, 0, (2, 3), False, True)
    pass_on((5, 0))
    pass_on((-5, 0))
    pass_on((3, 1))
    pass_on((-3, 1))
    tile(1, 1, (0, 1, 2, 3), True, False)
    all_arrived(4)
    all_arrived(5)
    tile(0, 1, (4, 5), False, True)
    for slot in ((6, 0), (6, 1), (5, 1), (-5, 1)):
        pass_on(slot)

    def grad_copy(source, slot, n, device, part):
        return pltpu.make_async_remote_copy(
            src_ref=source.at[pl.ds(part * PART, PART)],
            dst_ref=g_recv.at[slot, pl.ds(part * PART, PART)],
            send_sem=g_ss.at[n, part],
            recv_sem=g_rs.at[slot, part],
            device_id=device,
            device_id_type=MESH,
        )

    def grad_copies(source, slot, n, device):
        return [grad_copy(source, slot, n, device, part) for part in range(PARTS)]

    def pair_copy(slot, n):
        return pltpu.make_async_remote_copy(
            src_ref=txt_acc.at[slot],
            dst_ref=p_recv.at[n],
            send_sem=p_ss.at[n],
            recv_sem=p_rs.at[n],
            device_id=partner,
            device_id_type=MESH,
        )

    far_shift = side * (1 - inner_end) - 5 * side * inner_end
    early_shift = core * (2 - 8 * last) + (1 - core) * (8 * first - 2)
    late_shift = (1 - core) * (2 - 8 * last) + core * (8 * first - 2)
    early_slot = core * 3 * last + (1 - core) * (1 + 3 * first)
    late_slot = (1 - core) * 3 * last + core * (1 + 3 * first)
    grad_far = grad_copies(g_send.at[2], 2 + 4 * inner_end, 2, at(far_shift))
    grad_early = grad_copies(g_send.at[0], early_slot, 0, at(early_shift))
    grad_late = grad_copies(g_send.at[1], late_slot, 1, at(late_shift))
    grad_through = grad_copies(g_recv.at[3 + last], last, 3, at(8 * first - 8 * last))
    grad_far_through = grad_copies(g_recv.at[6], 5, 4, at(-8 * side))
    pair_own, pair_early, pair_late = pair_copy(1, 0), pair_copy(5 - core, 2 - core), pair_copy(4 + core, 1 + core)

    def grad_arrived(slot, part):
        grad_copy(g_send.at[0], slot, 0, partner, part).wait_recv()

    def pair_arrived(n):
        pair_copy(1, n).wait_recv()

    def image_copy(slot):
        pz, py = tree_parent(slot)
        rows = pl.ds(INDEX[slot] * IMG, IMG)
        return pltpu.make_async_remote_copy(
            src_ref=i_send.at[rows],
            dst_ref=i_recv.at[rows],
            send_sem=i_ss.at[INDEX[slot]],
            recv_sem=i_rs.at[INDEX[slot]],
            device_id=along_z(pz - slot[0], py != slot[1]),
            device_id_type=MESH,
        )

    def image_sum(slot):
        total = img_acc[pl.ds(INDEX[slot] * IMG, IMG), :]
        for kid in KIDS[slot]:
            image_copy(kid).wait_recv()
            total = total + i_recv[pl.ds(INDEX[kid] * IMG, IMG), :].astype(jnp.float32)
        return total

    def give_back(*slots):
        for slot in slots:
            i_send[pl.ds(INDEX[slot] * IMG, IMG), :] = image_sum(slot).astype(jnp.bfloat16)
            image_copy(slot).start()

    tile(2, 2, (0, 1, 2, 3, 4, 5), True, False)
    pair_early.start()
    pair_late.start()
    pair_own.start()
    all_arrived(6)
    tile(0, 2, (6,), False, True)
    g_send[2] = txt_acc[6].astype(jnp.bfloat16)
    for copy in grad_far:
        copy.start()
    give_back((6, 0), (5, 1), (6, 1), (-5, 1), (4, 1), (3, 1), (-3, 1), (1, 1), (-1, 1))
    pair_arrived(1 + core)
    for part in range(PARTS):
        rows = pl.ds(part * PART, PART)
        g_send[0, rows] = (txt_acc[2 + core, rows] + p_recv[1 + core, rows]).astype(jnp.bfloat16)
        grad_early[part].start()
    give_back((5, 0), (-5, 0), (3, 0), (-3, 0), (4, 0), (-4, 1), (-4, 0))

    pair_arrived(2 - core)
    for part in range(PARTS):
        rows = pl.ds(part * PART, PART)

        @pl.when(inner_end == 0)
        def _():
            grad_arrived(2, part)
            g_send[1, rows] = (
                txt_acc[3 - core, rows] + p_recv[2 - core, rows] + g_recv[2, rows].astype(jnp.float32)
            ).astype(jnp.bfloat16)

        @pl.when(inner_end == 1)
        def _():
            g_send[1, rows] = (txt_acc[3 - core, rows] + p_recv[2 - core, rows]).astype(jnp.bfloat16)

        grad_late[part].start()

    give_back((1, 0), (-1, 0))

    @pl.when(outer_end == 1)
    def _():
        for part in range(PARTS):
            grad_arrived(6, part)
            grad_far_through[part].start()

    def go_through():
        for part in range(PARTS):
            grad_arrived(3 + last, part)
            grad_through[part].start()

    early_through = first * core + last * (1 - core)
    late_through = first * (1 - core) + last * core

    @pl.when(early_through == 1)
    def _():
        go_through()

    give_back((2, 1), (-2, 1), (2, 0), (-2, 0), (0, 1))

    @pl.when(late_through == 1)
    def _():
        go_through()

    inverse, full = unit_rows(img_in[...])
    gi[...] = project_back(inverse, full, image_sum((0, 0)) * factor)
    store_img = pltpu.make_async_copy(gi, gi_hbm, out_sem.at[0])
    store_img.start()

    def store_txt(part):
        rows = pl.ds(part * PART, PART)
        return pltpu.make_async_copy(gt.at[rows], gt_hbm.at[rows], out_sem.at[1 + part])

    pair_arrived(0)
    for part in range(PARTS):
        rows = pl.ds(part * PART, PART)
        grad_arrived(0, part)
        grad_arrived(1, part)
        txt_acc[0, rows] += p_recv[0, rows] + (
            g_recv[0, rows].astype(jnp.float32) + g_recv[1, rows].astype(jnp.float32)
        )

        @pl.when(outer_end == 1)
        def _():
            grad_arrived(5, part)
            txt_acc[0, rows] += g_recv[5, rows].astype(jnp.float32)

        inverse, full = unit_rows(txt_in[rows, :])
        gt[rows, :] = project_back(inverse, full, txt_acc[0, rows] * factor)
        store_txt(part).start()

    for slot in SLOTS[1:]:
        gather_copy(slot).wait_send()
        image_copy(slot).wait_send()
    for copy in (pair_own, pair_early, pair_late):
        copy.wait_send()
    for copies in (text_partner, text_up, text_down, text_four, text_five, grad_far, grad_early, grad_late):
        for copy in copies:
            copy.wait_send()

    @pl.when(inner_end == 0)
    def _():
        for copy in text_far:
            copy.wait_send()

    @pl.when(outer_end == 1)
    def _():
        for copy in text_far_own + grad_far_through:
            copy.wait_send()

    @pl.when(through == 1)
    def _():
        for copy in text_through + grad_through:
            copy.wait_send()

    store_img.wait()
    for part in range(PARTS):
        store_txt(part).wait()


def local(images, texts, logit_scale, logit_bias):
    bf, f32 = jnp.bfloat16, jnp.float32
    dma = pltpu.SemaphoreType.DMA
    return pl.pallas_call(
        kernel,
        out_shape=(
            jax.ShapeDtypeStruct((IMG, D), f32),
            jax.ShapeDtypeStruct((TXT, D), f32),
        ),
        in_specs=[pl.BlockSpec(memory_space=pl.ANY)] * 4,
        out_specs=[pl.BlockSpec(memory_space=pl.ANY)] * 2,
        scratch_shapes=[
            pltpu.SMEM((1,), f32),
            pltpu.SMEM((1,), f32),
            pltpu.VMEM((IMG, D), bf),
            pltpu.VMEM((TXT, D), bf),
            pltpu.VMEM((NI * IMG, D), bf),
            pltpu.VMEM((9, TXT, D), bf),
            pltpu.VMEM((NI * IMG, D), f32),
            pltpu.VMEM((7, TXT, D), f32),
            pltpu.VMEM((NI * IMG, D), bf),
            pltpu.VMEM((NI * IMG, D), bf),
            pltpu.VMEM((3, TXT, D), bf),
            pltpu.VMEM((7, TXT, D), bf),
            pltpu.VMEM((3, TXT, D), f32),
            pltpu.VMEM((IMG, D), f32),
            pltpu.VMEM((TXT, D), f32),
            dma((4,)), dma((1 + PARTS,)),
            dma((NI,)), dma((NI,)),
            dma((8, PARTS)), dma((9, PARTS)),
            dma((NI,)), dma((NI,)),
            dma((5, PARTS)), dma((7, PARTS)),
            dma((3,)), dma((3,)),
        ],
        compiler_params=pltpu.CompilerParams(
            collective_id=0, has_side_effects=True, vmem_limit_bytes=48 << 20
        ),
        name="pair_gradients",
    )(logit_scale, logit_bias, images, texts)


def solution(mesh):
    return jax.shard_map(
        local,
        mesh=mesh,
        in_specs=(P(("outer", "inner"), None), P(("outer", "inner"), None), P(), P()),
        out_specs=(P(("outer", "inner"), None), P(("outer", "inner"), None)),
        check_vma=False,
    )
```

```python
import functools
import math

import jax
import jax.numpy as jnp
from jax import lax
from jax.experimental import pallas as pl
from jax.experimental.pallas import tpu as pltpu
from jax.sharding import PartitionSpec as P

MESH = pl.DeviceIdType.MESH
HALF = 3
D = 1152
IMG = 16
TXT = 128
NO, NI = 32, 24
NZ = 12

STAGE_Z = ((0, 1, -1, 2, -2), (3, -3, 4, -4), (5, -5, 6))
STAGES = tuple(tuple((dz, dy) for dy in (0, 1) for dz in zs) for zs in STAGE_Z)
SLOTS = tuple(slot for stage in STAGES for slot in stage)
INDEX = {slot: n for n, slot in enumerate(SLOTS)}
STAGE_AT = (0, 10, 18, 24)
PARTS = 4
PART = TXT // PARTS


def sign(value):
    return (value > 0) - (value < 0)


def gather_parent(slot):
    dz, dy = slot
    if dz == 0:
        return (0, 0)
    if dz == 6:
        return (4, 0) if dy == 0 else (-4, 1)
    if dz in (2, -2):
        return (0, 0)
    return (sign(dz) * ((abs(dz) - 1) // 2 * 2), dy)


def return_parent(slot):
    dz, dy = slot
    if dz == 6:
        return (3, 0) if dy == 0 else (-3, 0)
    if dy and abs(dz) < 5:
        return (dz, 0)
    return (sign(dz) * ((abs(dz) - 1) // 3 * 3), 0)


def kids_of(parent):
    return {
        slot: tuple(
            sorted((kid for kid in SLOTS[1:] if parent(kid) == slot), key=lambda kid: (kid[1] == slot[1], -abs(kid[0])))
        )
        for slot in SLOTS
    }


def move(start, end):
    dz = (end[0] - start[0]) % NZ
    return (dz - NZ if dz > NZ // 2 else dz, (end[1] - start[1]) % 2)


GATHER_KIDS = kids_of(gather_parent)
RETURN_KIDS = kids_of(return_parent)
MOVES = sorted(
    {move(gather_parent(slot), slot) for slot in SLOTS[1:]}
    | {move(slot, gather_parent(slot)) for slot in SLOTS[1:]}
    | {move(slot, return_parent(slot)) for slot in SLOTS[1:]}
    | {move(return_parent(slot), slot) for slot in SLOTS[1:]}
)


def unit_rows(values):
    widened = values.astype(jnp.float32)
    inverse = lax.rsqrt(jnp.sum(widened * widened, axis=-1, keepdims=True) + 1e-06)
    return inverse, widened * inverse


def project_back(inverse, unit_full, gradient):
    along = jnp.sum(unit_full * gradient, axis=-1, keepdims=True)
    return inverse * (gradient - unit_full * along)


def kernel(
    scale_hbm, bias_hbm, img_hbm, txt_hbm, gi_hbm, gt_hbm,
    scale, bias, img_in, txt_in, img, txt, img_acc, txt_acc,
    i_send, i_recv, g_send, g_recv, p_send, p_recv, gi, gt,
    in_sem, out_sem, ag_ss, ag_rs, t_ss, t_rs, i_ss, i_rs, g_ss, g_rs, p_ss, p_rs,
):
    o = lax.axis_index("outer")
    i = lax.axis_index("inner")
    core = o % 2
    x = (o // 2) % 4
    z = i // 2
    yl = i % 2
    divisor = 1.0 / math.sqrt((2 * HALF + 1) * NI * TXT)

    def along_z(dz, flip):
        return (o, ((z + dz + NZ) % NZ) * 2 + (1 - yl if flip else yl))

    def at(shift):
        return ((o + shift + NO) % NO, i)

    last_x = x // 3
    first_x = (3 - x) // 3
    last = last_x * yl
    first = first_x * yl
    through = last + first
    inner_end = last_x * core + first_x * (1 - core)
    outer_end = (x // 2) * (1 - x % 2) * core + (x % 2) * (1 - x // 2) * (1 - core)
    side = 2 * core - 1

    barrier = pltpu.get_barrier_semaphore()

    def greet(device):
        pl.semaphore_signal(barrier, inc=1, device_id=device, device_id_type=MESH)

    peers = [along_z(dz, flip) for dz, flip in MOVES]
    peers += [at(1 - 2 * core), at(side), at(2), at(-2)]
    for peer in peers:
        greet(peer)

    @pl.when(through == 1)
    def _():
        greet(at(6 * first_x - 6 * last_x))
        greet(at(8))
        greet(at(-8))

    @pl.when(inner_end == 1)
    def _():
        greet(at(3 * side))
        greet(at(-5 * side))

    @pl.when(outer_end == 1)
    def _():
        greet(at(3 * side))
        greet(at(-5 * side))
        greet(at(8))
        greet(at(-8))

    loads = [
        pltpu.make_async_copy(source, target, in_sem.at[n])
        for n, (source, target) in enumerate(
            ((img_hbm, img_in), (txt_hbm, txt_in), (scale_hbm, scale), (bias_hbm, bias))
        )
    ]
    for load in loads:
        load.start()
    loads[0].wait()
    _, full = unit_rows(img_in[...])
    img[0:IMG, :] = full.astype(jnp.bfloat16)

    pl.semaphore_wait(barrier, len(peers) + 3 * through + 2 * inner_end + 4 * outer_end)

    def gather_copy(kid):
        parent = gather_parent(kid)
        a, b = INDEX[parent], INDEX[kid]
        return pltpu.make_async_remote_copy(
            src_ref=img.at[a * IMG:(a + 1) * IMG],
            dst_ref=img.at[b * IMG:(b + 1) * IMG],
            send_sem=ag_ss.at[b],
            recv_sem=ag_rs.at[b],
            device_id=along_z(*move(parent, kid)),
            device_id_type=MESH,
        )

    def pass_on(slot):
        if slot != (0, 0):
            gather_copy(slot).wait_recv()
        for kid in GATHER_KIDS[slot]:
            gather_copy(kid).start()

    def text_copy(source, slot, n, device, part):
        rows = pl.ds(part * PART, PART)
        return pltpu.make_async_remote_copy(
            src_ref=txt.at[source, rows],
            dst_ref=txt.at[slot, rows],
            send_sem=t_ss.at[n, part],
            recv_sem=t_rs.at[slot, part],
            device_id=device,
            device_id_type=MESH,
        )

    def text_copies(source, slot, n, device):
        return [text_copy(source, slot, n, device, part) for part in range(PARTS)]

    partner = at(1 - 2 * core)
    up = at(2 - 8 * last)
    down = at(8 * first - 2)
    text_partner = text_copies(0, 1, 1, partner)
    text_up = text_copies(0, 2 + 5 * last, 2, up)
    text_down = text_copies(0, 3 + 5 * first, 3, down)
    text_four = text_copies(2, 4, 4, partner)
    text_five = text_copies(3, 5, 5, partner)
    text_far = text_copies(3 - core, 6, 6, at(side))
    text_far_own = text_copies(0, 6, 0, at(3 * side))
    text_through = text_copies(7 + last, 2 + last, 7, at(8 * first - 8 * last))

    def text_arrived(slot, part):
        text_copy(0, slot, 0, partner, part).wait_recv()

    def all_arrived(slot):
        for part in range(PARTS):
            text_arrived(slot, part)

    pass_on((0, 0))
    loads[1].wait()
    _, full = unit_rows(txt_in[...])
    txt[0] = full.astype(jnp.bfloat16)
    for part in range(PARTS):
        text_up[part].start()
        text_down[part].start()

    @pl.when(outer_end == 1)
    def _():
        for part in range(PARTS):
            text_far_own[part].start()

    for part in range(PARTS):
        text_partner[part].start()
    pass_on((0, 1))
    loads[2].wait()
    loads[3].wait()
    factor = scale[0]
    offset = bias[0]

    def tile(first_stage, last_stage, slots, first_rows, first_cols):
        r0, r1 = STAGE_AT[first_stage] * IMG, STAGE_AT[last_stage + 1] * IMG
        s0, n = slots[0], len(slots)
        rows = img[r0:r1, :]
        cols = txt[s0:s0 + n].reshape(n * TXT, D)
        logits = lax.dot_general(
            cols, rows, (((1,), (1,)), ((), ())), preferred_element_type=jnp.float32
        ) * factor + offset
        if r0 == 0 and s0 == 0:
            shape = (n * TXT, r1 - r0)
            t = lax.broadcasted_iota(jnp.int32, shape, 0)
            r = lax.broadcasted_iota(jnp.int32, shape, 1)
            matched = jnp.logical_and(r == t, r < IMG)
            label = jnp.where(matched, 1.0, -1.0)
            weights = -label / (1.0 + jnp.exp(label * logits)) * divisor
        else:
            weights = divisor / (1.0 + jnp.exp(-logits))
        weights = weights.astype(jnp.bfloat16)
        text_part = jnp.dot(weights, rows, preferred_element_type=jnp.float32).reshape(n, TXT, D)
        image_part = lax.dot_general(
            weights, cols, (((0,), (0,)), ((), ())), preferred_element_type=jnp.float32
        )
        if first_rows:
            img_acc[r0:r1, :] = image_part
        else:
            img_acc[r0:r1, :] += image_part
        if first_cols:
            txt_acc[s0:s0 + n] = text_part
        else:
            txt_acc[s0:s0 + n] += text_part

    ahead = 1 - z // (NZ // 2)
    plus = ((z + 9) % NZ) // (NZ // 2)

    def pass_side(plus_side, *places):
        for value, side_sign in ((plus_side, 1), (1 - plus_side, -1)):

            @pl.when(value == 1)
            def _():
                for dz in places:
                    pass_on((side_sign * dz, 0))
                    pass_on((side_sign * dz, 1))

    def relay_texts():
        @pl.when(through == 1)
        def _():
            for part in range(PARTS):
                text_arrived(7 + last, part)
                text_through[part].start()

    def pass_texts():
        for part in range(PARTS):
            text_arrived(2, part)
            text_arrived(3, part)

            @pl.when(inner_end == 0)
            def _():
                text_far[part].start()

            text_four[part].start()
            text_five[part].start()

    @pl.when(ahead == 1)
    def _():
        relay_texts()
        pass_texts()

    pass_side(1 - plus, 2)
    pass_side(plus, 2)
    pass_side(1 - plus, 4)

    @pl.when(ahead == 1)
    def _():
        pass_side(plus, 4)

    @pl.when(ahead == 0)
    def _():
        relay_texts()

    for slot in ((1, 0), (-1, 0), (1, 1), (-1, 1)):
        pass_on(slot)
    all_arrived(1)
    tile(0, 0, (0, 1), True, True)

    @pl.when(ahead == 0)
    def _():
        pass_side(plus, 4)
        pass_texts()

    tile(0, 0, (2, 3), False, True)
    for slot in ((3, 0), (-3, 0), (3, 1), (-3, 1)):
        pass_on(slot)
    tile(1, 1, (0, 1, 2, 3), True, False)
    all_arrived(4)
    all_arrived(5)
    tile(0, 1, (4, 5), False, True)
    all_arrived(6)
    tile(0, 1, (6,), False, True)

    def grad_copy(source, slot, n, device, part):
        return pltpu.make_async_remote_copy(
            src_ref=source.at[pl.ds(part * PART, PART)],
            dst_ref=g_recv.at[slot, pl.ds(part * PART, PART)],
            send_sem=g_ss.at[n, part],
            recv_sem=g_rs.at[slot, part],
            device_id=device,
            device_id_type=MESH,
        )

    def grad_copies(source, slot, n, device):
        return [grad_copy(source, slot, n, device, part) for part in range(PARTS)]

    def pair_copy(n):
        return pltpu.make_async_remote_copy(
            src_ref=p_send.at[n],
            dst_ref=p_recv.at[n],
            send_sem=p_ss.at[n],
            recv_sem=p_rs.at[n],
            device_id=partner,
            device_id_type=MESH,
        )

    far_shift = side * (1 - inner_end) - 5 * side * inner_end
    early_shift = core * (2 - 8 * last) + (1 - core) * (8 * first - 2)
    late_shift = (1 - core) * (2 - 8 * last) + core * (8 * first - 2)
    early_slot = core * 3 * last + (1 - core) * (1 + 3 * first)
    late_slot = (1 - core) * 3 * last + core * (1 + 3 * first)
    grad_far = grad_copies(g_send.at[2], 2 + 4 * inner_end, 2, at(far_shift))
    grad_early = grad_copies(g_send.at[0], early_slot, 0, at(early_shift))
    grad_late = grad_copies(g_send.at[1], late_slot, 1, at(late_shift))
    grad_through = grad_copies(g_recv.at[3 + last], last, 3, at(8 * first - 8 * last))
    grad_far_through = grad_copies(g_recv.at[6], 5, 4, at(-8 * side))
    pair_own, pair_early, pair_late = pair_copy(0), pair_copy(2 - core), pair_copy(1 + core)

    def grad_arrived(slot, part):
        grad_copy(g_send.at[0], slot, 0, partner, part).wait_recv()

    def pair_arrived(n):
        pair_copy(n).wait_recv()

    def image_copy(slot):
        rows = pl.ds(INDEX[slot] * IMG, IMG)
        return pltpu.make_async_remote_copy(
            src_ref=i_send.at[rows],
            dst_ref=i_recv.at[rows],
            send_sem=i_ss.at[INDEX[slot]],
            recv_sem=i_rs.at[INDEX[slot]],
            device_id=along_z(*move(slot, return_parent(slot))),
            device_id_type=MESH,
        )

    def image_sum(slot):
        total = img_acc[pl.ds(INDEX[slot] * IMG, IMG), :]
        for kid in RETURN_KIDS[slot]:
            image_copy(kid).wait_recv()
            total = total + i_recv[pl.ds(INDEX[kid] * IMG, IMG), :].astype(jnp.float32)
        return total

    def give_back(*slots):
        for slot in slots:
            i_send[pl.ds(INDEX[slot] * IMG, IMG), :] = image_sum(slot).astype(jnp.bfloat16)
            image_copy(slot).start()

    give_back((0, 1), (4, 1), (-4, 1), (3, 1), (-3, 1), (2, 1), (-2, 1), (1, 1), (-1, 1))
    for slot in STAGES[2]:
        pass_on(slot)
    tile(2, 2, (4, 5, 6), True, False)
    g_send[2] = txt_acc[6].astype(jnp.bfloat16)
    for copy in grad_far:
        copy.start()
    p_send[2 - core] = txt_acc[5 - core].astype(jnp.bfloat16)
    pair_early.start()
    p_send[1 + core] = txt_acc[4 + core].astype(jnp.bfloat16)
    pair_late.start()
    tile(2, 2, (0, 1, 2, 3), False, False)
    give_back((6, 0), (6, 1), (5, 1), (-5, 1), (5, 0), (-5, 0), (4, 0), (-4, 0))
    pair_arrived(1 + core)
    for part in range(PARTS):
        rows = pl.ds(part * PART, PART)
        g_send[0, rows] = (txt_acc[2 + core, rows] + p_recv[1 + core, rows].astype(jnp.float32)).astype(jnp.bfloat16)
        grad_early[part].start()
    p_send[0] = txt_acc[1].astype(jnp.bfloat16)
    pair_own.start()
    give_back((2, 0), (-2, 0), (1, 0), (-1, 0))

    pair_arrived(2 - core)
    for part in range(PARTS):
        rows = pl.ds(part * PART, PART)

        @pl.when(inner_end == 0)
        def _():
            grad_arrived(2, part)
            g_send[1, rows] = (
                txt_acc[3 - core, rows]
                + p_recv[2 - core, rows].astype(jnp.float32)
                + g_recv[2, rows].astype(jnp.float32)
            ).astype(jnp.bfloat16)

        @pl.when(inner_end == 1)
        def _():
            g_send[1, rows] = (
                txt_acc[3 - core, rows] + p_recv[2 - core, rows].astype(jnp.float32)
            ).astype(jnp.bfloat16)

        grad_late[part].start()

    give_back((3, 0), (-3, 0))

    @pl.when(outer_end == 1)
    def _():
        for part in range(PARTS):
            grad_arrived(6, part)
            grad_far_through[part].start()

    def go_through():
        for part in range(PARTS):
            grad_arrived(3 + last, part)
            grad_through[part].start()

    early_through = first * core + last * (1 - core)
    late_through = first * (1 - core) + last * core

    @pl.when(early_through == 1)
    def _():
        go_through()


    @pl.when(late_through == 1)
    def _():
        go_through()

    inverse, full = unit_rows(img_in[...])
    gi[...] = project_back(inverse, full, image_sum((0, 0)) * factor)
    store_img = pltpu.make_async_copy(gi, gi_hbm, out_sem.at[0])
    store_img.start()

    def store_txt(part):
        rows = pl.ds(part * PART, PART)
        return pltpu.make_async_copy(gt.at[rows], gt_hbm.at[rows], out_sem.at[1 + part])

    pair_arrived(0)
    for part in range(PARTS):
        rows = pl.ds(part * PART, PART)
        grad_arrived(0, part)
        grad_arrived(1, part)
        txt_acc[0, rows] += p_recv[0, rows].astype(jnp.float32) + (
            g_recv[0, rows].astype(jnp.float32) + g_recv[1, rows].astype(jnp.float32)
        )

        @pl.when(outer_end == 1)
        def _():
            grad_arrived(5, part)
            txt_acc[0, rows] += g_recv[5, rows].astype(jnp.float32)

        inverse, full = unit_rows(txt_in[rows, :])
        gt[rows, :] = project_back(inverse, full, txt_acc[0, rows] * factor)
        store_txt(part).start()

    for slot in SLOTS[1:]:
        gather_copy(slot).wait_send()
        image_copy(slot).wait_send()
    for copy in (pair_own, pair_early, pair_late):
        copy.wait_send()
    for copies in (text_partner, text_up, text_down, text_four, text_five, grad_far, grad_early, grad_late):
        for copy in copies:
            copy.wait_send()

    @pl.when(inner_end == 0)
    def _():
        for copy in text_far:
            copy.wait_send()

    @pl.when(outer_end == 1)
    def _():
        for copy in text_far_own + grad_far_through:
            copy.wait_send()

    @pl.when(through == 1)
    def _():
        for copy in text_through + grad_through:
            copy.wait_send()

    store_img.wait()
    for part in range(PARTS):
        store_txt(part).wait()


def local(images, texts, logit_scale, logit_bias):
    bf, f32 = jnp.bfloat16, jnp.float32
    dma = pltpu.SemaphoreType.DMA
    return pl.pallas_call(
        kernel,
        out_shape=(
            jax.ShapeDtypeStruct((IMG, D), f32),
            jax.ShapeDtypeStruct((TXT, D), f32),
        ),
        in_specs=[pl.BlockSpec(memory_space=pl.ANY)] * 4,
        out_specs=[pl.BlockSpec(memory_space=pl.ANY)] * 2,
        scratch_shapes=[
            pltpu.SMEM((1,), f32),
            pltpu.SMEM((1,), f32),
            pltpu.VMEM((IMG, D), bf),
            pltpu.VMEM((TXT, D), bf),
            pltpu.VMEM((NI * IMG, D), bf),
            pltpu.VMEM((9, TXT, D), bf),
            pltpu.VMEM((NI * IMG, D), f32),
            pltpu.VMEM((7, TXT, D), f32),
            pltpu.VMEM((NI * IMG, D), bf),
            pltpu.VMEM((NI * IMG, D), bf),
            pltpu.VMEM((3, TXT, D), bf),
            pltpu.VMEM((7, TXT, D), bf),
            pltpu.VMEM((3, TXT, D), bf),
            pltpu.VMEM((3, TXT, D), bf),
            pltpu.VMEM((IMG, D), f32),
            pltpu.VMEM((TXT, D), f32),
            dma((4,)), dma((1 + PARTS,)),
            dma((NI,)), dma((NI,)),
            dma((8, PARTS)), dma((9, PARTS)),
            dma((NI,)), dma((NI,)),
            dma((5, PARTS)), dma((7, PARTS)),
            dma((3,)), dma((3,)),
        ],
        compiler_params=pltpu.CompilerParams(
            collective_id=0, has_side_effects=True, vmem_limit_bytes=48 << 20
        ),
        name="pair_gradients",
    )(logit_scale, logit_bias, images, texts)


def solution(mesh):
    return jax.shard_map(
        local,
        mesh=mesh,
        in_specs=(P(("outer", "inner"), None), P(("outer", "inner"), None), P(), P()),
        out_specs=(P(("outer", "inner"), None), P(("outer", "inner"), None)),
        check_vma=False,
    )
```

```python
import functools
import math

import jax
import jax.numpy as jnp
from jax import lax
from jax.experimental import pallas as pl
from jax.experimental.pallas import tpu as pltpu
from jax.sharding import PartitionSpec as P

MESH = pl.DeviceIdType.MESH
HALF = 3
D = 1152
IMG = 16
TXT = 128
NO, NI = 32, 24
NZ = 12

STAGE_Z = ((0, 1, -1, 2, -2), (3, -3, 4, -4), (5, -5, 6))
STAGES = tuple(tuple((dz, dy) for dy in (0, 1) for dz in zs) for zs in STAGE_Z)
SLOTS = tuple(slot for stage in STAGES for slot in stage)
INDEX = {slot: n for n, slot in enumerate(SLOTS)}
STAGE_AT = (0, 10, 18, 24)
PARTS = 4
PART = TXT // PARTS


def sign(value):
    return (value > 0) - (value < 0)


def gather_parent(slot):
    dz, dy = slot
    if dz == 0:
        return (0, 0)
    if dz == 6:
        return (4, 0) if dy == 0 else (-4, 1)
    if dz in (2, -2):
        return (0, 0)
    return (sign(dz) * ((abs(dz) - 1) // 2 * 2), dy)


def return_parent(slot):
    dz, dy = slot
    if dz == 6:
        return (3, 0) if dy == 0 else (-3, 0)
    if dy and abs(dz) < 5:
        return (dz, 0)
    return (sign(dz) * ((abs(dz) - 1) // 3 * 3), 0)


def kids_of(parent):
    return {
        slot: tuple(
            sorted((kid for kid in SLOTS[1:] if parent(kid) == slot), key=lambda kid: (kid[1] == slot[1], -abs(kid[0])))
        )
        for slot in SLOTS
    }


def move(start, end):
    dz = (end[0] - start[0]) % NZ
    return (dz - NZ if dz > NZ // 2 else dz, (end[1] - start[1]) % 2)


GATHER_KIDS = kids_of(gather_parent)
RETURN_KIDS = kids_of(return_parent)
MOVES = sorted(
    {move(gather_parent(slot), slot) for slot in SLOTS[1:]}
    | {move(slot, gather_parent(slot)) for slot in SLOTS[1:]}
    | {move(slot, return_parent(slot)) for slot in SLOTS[1:]}
    | {move(return_parent(slot), slot) for slot in SLOTS[1:]}
)


def unit_rows(values):
    widened = values.astype(jnp.float32)
    inverse = lax.rsqrt(jnp.sum(widened * widened, axis=-1, keepdims=True) + 1e-06)
    return inverse, widened * inverse


def project_back(inverse, unit_full, gradient):
    along = jnp.sum(unit_full * gradient, axis=-1, keepdims=True)
    return inverse * (gradient - unit_full * along)


def kernel(
    scale_hbm, bias_hbm, img_hbm, txt_hbm, gi_hbm, gt_hbm,
    scale, bias, img_in, txt_in, img, txt, img_acc, txt_acc,
    i_send, i_recv, g_send, g_recv, p_send, p_recv, gi, gt,
    in_sem, out_sem, ag_ss, ag_rs, t_ss, t_rs, i_ss, i_rs, g_ss, g_rs, p_ss, p_rs,
):
    o = lax.axis_index("outer")
    i = lax.axis_index("inner")
    core = o % 2
    x = (o // 2) % 4
    z = i // 2
    yl = i % 2
    divisor = 1.0 / math.sqrt((2 * HALF + 1) * NI * TXT)

    def along_z(dz, flip):
        return (o, ((z + dz + NZ) % NZ) * 2 + (1 - yl if flip else yl))

    def at(shift):
        return ((o + shift + NO) % NO, i)

    last_x = x // 3
    first_x = (3 - x) // 3
    last = last_x * yl
    first = first_x * yl
    through = last + first
    inner_end = last_x * core + first_x * (1 - core)
    outer_end = (x // 2) * (1 - x % 2) * core + (x % 2) * (1 - x // 2) * (1 - core)
    side = 2 * core - 1

    barrier = pltpu.get_barrier_semaphore()

    def greet(device):
        pl.semaphore_signal(barrier, inc=1, device_id=device, device_id_type=MESH)

    peers = [along_z(dz, flip) for dz, flip in MOVES]
    peers += [at(1 - 2 * core), at(side), at(2), at(-2)]
    for peer in peers:
        greet(peer)

    @pl.when(through == 1)
    def _():
        greet(at(6 * first_x - 6 * last_x))
        greet(at(8))
        greet(at(-8))

    @pl.when(inner_end == 1)
    def _():
        greet(at(3 * side))
        greet(at(-5 * side))

    @pl.when(outer_end == 1)
    def _():
        greet(at(3 * side))
        greet(at(-5 * side))
        greet(at(8))
        greet(at(-8))

    loads = [
        pltpu.make_async_copy(source, target, in_sem.at[n])
        for n, (source, target) in enumerate(
            ((img_hbm, img_in), (txt_hbm, txt_in), (scale_hbm, scale), (bias_hbm, bias))
        )
    ]
    for load in loads:
        load.start()
    loads[0].wait()
    _, full = unit_rows(img_in[...])
    img[0:IMG, :] = full.astype(jnp.bfloat16)

    pl.semaphore_wait(barrier, len(peers) + 3 * through + 2 * inner_end + 4 * outer_end)

    def gather_copy(kid):
        parent = gather_parent(kid)
        a, b = INDEX[parent], INDEX[kid]
        return pltpu.make_async_remote_copy(
            src_ref=img.at[a * IMG:(a + 1) * IMG],
            dst_ref=img.at[b * IMG:(b + 1) * IMG],
            send_sem=ag_ss.at[b],
            recv_sem=ag_rs.at[b],
            device_id=along_z(*move(parent, kid)),
            device_id_type=MESH,
        )

    def pass_on(slot):
        if slot != (0, 0):
            gather_copy(slot).wait_recv()
        for kid in GATHER_KIDS[slot]:
            gather_copy(kid).start()

    def text_copy(source, slot, n, device, part):
        rows = pl.ds(part * PART, PART)
        return pltpu.make_async_remote_copy(
            src_ref=txt.at[source, rows],
            dst_ref=txt.at[slot, rows],
            send_sem=t_ss.at[n, part],
            recv_sem=t_rs.at[slot, part],
            device_id=device,
            device_id_type=MESH,
        )

    def text_copies(source, slot, n, device):
        return [text_copy(source, slot, n, device, part) for part in range(PARTS)]

    partner = at(1 - 2 * core)
    up = at(2 - 8 * last)
    down = at(8 * first - 2)
    text_partner = text_copies(0, 1, 1, partner)
    text_up = text_copies(0, 2 + 5 * last, 2, up)
    text_down = text_copies(0, 3 + 5 * first, 3, down)
    text_four = text_copies(2, 4, 4, partner)
    text_five = text_copies(3, 5, 5, partner)
    text_far = text_copies(3 - core, 6, 6, at(side))
    text_far_own = text_copies(0, 6, 0, at(3 * side))
    text_through = text_copies(7 + last, 2 + last, 7, at(8 * first - 8 * last))

    def text_arrived(slot, part):
        text_copy(0, slot, 0, partner, part).wait_recv()

    def all_arrived(slot):
        for part in range(PARTS):
            text_arrived(slot, part)

    pass_on((0, 0))
    loads[1].wait()
    _, full = unit_rows(txt_in[...])
    txt[0] = full.astype(jnp.bfloat16)
    for part in range(PARTS):
        text_up[part].start()
        text_down[part].start()

    @pl.when(outer_end == 1)
    def _():
        for part in range(PARTS):
            text_far_own[part].start()

    for part in range(PARTS):
        text_partner[part].start()
    pass_on((0, 1))
    loads[2].wait()
    loads[3].wait()
    factor = scale[0]
    offset = bias[0]

    def tile(first_stage, last_stage, slots, first_rows, first_cols):
        r0, r1 = STAGE_AT[first_stage] * IMG, STAGE_AT[last_stage + 1] * IMG
        s0, n = slots[0], len(slots)
        rows = img[r0:r1, :]
        cols = txt[s0:s0 + n].reshape(n * TXT, D)
        logits = lax.dot_general(
            cols, rows, (((1,), (1,)), ((), ())), preferred_element_type=jnp.float32
        ) * factor + offset
        if r0 == 0 and s0 == 0:
            shape = (n * TXT, r1 - r0)
            t = lax.broadcasted_iota(jnp.int32, shape, 0)
            r = lax.broadcasted_iota(jnp.int32, shape, 1)
            matched = jnp.logical_and(r == t, r < IMG)
            label = jnp.where(matched, 1.0, -1.0)
            weights = -label / (1.0 + jnp.exp(label * logits)) * divisor
        else:
            weights = divisor / (1.0 + jnp.exp(-logits))
        weights = weights.astype(jnp.bfloat16)
        text_part = jnp.dot(weights, rows, preferred_element_type=jnp.float32).reshape(n, TXT, D)
        image_part = lax.dot_general(
            weights, cols, (((0,), (0,)), ((), ())), preferred_element_type=jnp.float32
        )
        if first_rows:
            img_acc[r0:r1, :] = image_part
        else:
            img_acc[r0:r1, :] += image_part
        if first_cols:
            txt_acc[s0:s0 + n] = text_part
        else:
            txt_acc[s0:s0 + n] += text_part

    for slot in ((2, 0), (-2, 0), (2, 1), (-2, 1)):
        pass_on(slot)

    @pl.when(through == 1)
    def _():
        for part in range(PARTS):
            text_arrived(7 + last, part)
            text_through[part].start()

    for slot in ((1, 0), (-1, 0), (1, 1), (-1, 1)):
        pass_on(slot)
    all_arrived(1)
    tile(0, 0, (0, 1), True, True)
    for slot in ((4, 0), (-4, 0), (4, 1), (-4, 1)):
        pass_on(slot)
    for part in range(PARTS):
        text_arrived(2, part)
        text_arrived(3, part)

        @pl.when(inner_end == 0)
        def _():
            text_far[part].start()

        text_four[part].start()
        text_five[part].start()
    tile(0, 0, (2, 3), False, True)
    for slot in ((3, 0), (-3, 0), (3, 1), (-3, 1)):
        pass_on(slot)
    tile(1, 1, (0, 1, 2, 3), True, False)
    all_arrived(4)
    all_arrived(5)
    tile(0, 1, (4, 5), False, True)
    all_arrived(6)
    tile(0, 1, (6,), False, True)

    def grad_copy(source, slot, n, device, part):
        return pltpu.make_async_remote_copy(
            src_ref=source.at[pl.ds(part * PART, PART)],
            dst_ref=g_recv.at[slot, pl.ds(part * PART, PART)],
            send_sem=g_ss.at[n, part],
            recv_sem=g_rs.at[slot, part],
            device_id=device,
            device_id_type=MESH,
        )

    def grad_copies(source, slot, n, device):
        return [grad_copy(source, slot, n, device, part) for part in range(PARTS)]

    def pair_copy(n):
        return pltpu.make_async_remote_copy(
            src_ref=p_send.at[n],
            dst_ref=p_recv.at[n],
            send_sem=p_ss.at[n],
            recv_sem=p_rs.at[n],
            device_id=partner,
            device_id_type=MESH,
        )

    far_shift = side * (1 - inner_end) - 5 * side * inner_end
    early_shift = core * (2 - 8 * last) + (1 - core) * (8 * first - 2)
    late_shift = (1 - core) * (2 - 8 * last) + core * (8 * first - 2)
    early_slot = core * 3 * last + (1 - core) * (1 + 3 * first)
    late_slot = (1 - core) * 3 * last + core * (1 + 3 * first)
    grad_far = grad_copies(g_send.at[2], 2 + 4 * inner_end, 2, at(far_shift))
    grad_early = grad_copies(g_send.at[0], early_slot, 0, at(early_shift))
    grad_late = grad_copies(g_send.at[1], late_slot, 1, at(late_shift))
    grad_through = grad_copies(g_recv.at[3 + last], last, 3, at(8 * first - 8 * last))
    grad_far_through = grad_copies(g_recv.at[6], 5, 4, at(-8 * side))
    pair_own, pair_early, pair_late = pair_copy(0), pair_copy(2 - core), pair_copy(1 + core)

    def grad_arrived(slot, part):
        grad_copy(g_send.at[0], slot, 0, partner, part).wait_recv()

    def pair_arrived(n):
        pair_copy(n).wait_recv()

    def image_copy(slot):
        rows = pl.ds(INDEX[slot] * IMG, IMG)
        return pltpu.make_async_remote_copy(
            src_ref=i_send.at[rows],
            dst_ref=i_recv.at[rows],
            send_sem=i_ss.at[INDEX[slot]],
            recv_sem=i_rs.at[INDEX[slot]],
            device_id=along_z(*move(slot, return_parent(slot))),
            device_id_type=MESH,
        )

    def image_sum(slot):
        total = img_acc[pl.ds(INDEX[slot] * IMG, IMG), :]
        for kid in RETURN_KIDS[slot]:
            image_copy(kid).wait_recv()
            total = total + i_recv[pl.ds(INDEX[kid] * IMG, IMG), :].astype(jnp.float32)
        return total

    def give_back(*slots):
        for slot in slots:
            i_send[pl.ds(INDEX[slot] * IMG, IMG), :] = image_sum(slot).astype(jnp.bfloat16)
            image_copy(slot).start()

    give_back((0, 1), (4, 1), (-4, 1), (3, 1), (-3, 1), (2, 1), (-2, 1), (1, 1), (-1, 1))
    for slot in STAGES[2]:
        pass_on(slot)
    tile(2, 2, (4, 5, 6), True, False)
    g_send[2] = txt_acc[6].astype(jnp.bfloat16)
    for copy in grad_far:
        copy.start()
    p_send[2 - core] = txt_acc[5 - core].astype(jnp.bfloat16)
    pair_early.start()
    p_send[1 + core] = txt_acc[4 + core].astype(jnp.bfloat16)
    pair_late.start()
    tile(2, 2, (0, 1, 2, 3), False, False)
    give_back((6, 0), (6, 1), (5, 1), (-5, 1), (5, 0), (-5, 0), (4, 0), (-4, 0))
    pair_arrived(1 + core)
    for part in range(PARTS):
        rows = pl.ds(part * PART, PART)
        g_send[0, rows] = (txt_acc[2 + core, rows] + p_recv[1 + core, rows].astype(jnp.float32)).astype(jnp.bfloat16)
        grad_early[part].start()
    p_send[0] = txt_acc[1].astype(jnp.bfloat16)
    pair_own.start()
    give_back((2, 0), (-2, 0), (1, 0), (-1, 0))

    pair_arrived(2 - core)
    for part in range(PARTS):
        rows = pl.ds(part * PART, PART)

        @pl.when(inner_end == 0)
        def _():
            grad_arrived(2, part)
            g_send[1, rows] = (
                txt_acc[3 - core, rows]
                + p_recv[2 - core, rows].astype(jnp.float32)
                + g_recv[2, rows].astype(jnp.float32)
            ).astype(jnp.bfloat16)

        @pl.when(inner_end == 1)
        def _():
            g_send[1, rows] = (
                txt_acc[3 - core, rows] + p_recv[2 - core, rows].astype(jnp.float32)
            ).astype(jnp.bfloat16)

        grad_late[part].start()

    give_back((3, 0), (-3, 0))

    @pl.when(outer_end == 1)
    def _():
        for part in range(PARTS):
            grad_arrived(6, part)
            grad_far_through[part].start()

    def go_through():
        for part in range(PARTS):
            grad_arrived(3 + last, part)
            grad_through[part].start()

    early_through = first * core + last * (1 - core)
    late_through = first * (1 - core) + last * core

    @pl.when(early_through == 1)
    def _():
        go_through()


    @pl.when(late_through == 1)
    def _():
        go_through()

    inverse, full = unit_rows(img_in[...])
    gi[...] = project_back(inverse, full, image_sum((0, 0)) * factor)
    store_img = pltpu.make_async_copy(gi, gi_hbm, out_sem.at[0])
    store_img.start()

    def store_txt(part):
        rows = pl.ds(part * PART, PART)
        return pltpu.make_async_copy(gt.at[rows], gt_hbm.at[rows], out_sem.at[1 + part])

    pair_arrived(0)
    for part in range(PARTS):
        rows = pl.ds(part * PART, PART)
        grad_arrived(0, part)
        grad_arrived(1, part)
        txt_acc[0, rows] += p_recv[0, rows].astype(jnp.float32) + (
            g_recv[0, rows].astype(jnp.float32) + g_recv[1, rows].astype(jnp.float32)
        )

        @pl.when(outer_end == 1)
        def _():
            grad_arrived(5, part)
            txt_acc[0, rows] += g_recv[5, rows].astype(jnp.float32)

        inverse, full = unit_rows(txt_in[rows, :])
        gt[rows, :] = project_back(inverse, full, txt_acc[0, rows] * factor)
        store_txt(part).start()

    for slot in SLOTS[1:]:
        gather_copy(slot).wait_send()
        image_copy(slot).wait_send()
    for copy in (pair_own, pair_early, pair_late):
        copy.wait_send()
    for copies in (text_partner, text_up, text_down, text_four, text_five, grad_far, grad_early, grad_late):
        for copy in copies:
            copy.wait_send()

    @pl.when(inner_end == 0)
    def _():
        for copy in text_far:
            copy.wait_send()

    @pl.when(outer_end == 1)
    def _():
        for copy in text_far_own + grad_far_through:
            copy.wait_send()

    @pl.when(through == 1)
    def _():
        for copy in text_through + grad_through:
            copy.wait_send()

    store_img.wait()
    for part in range(PARTS):
        store_txt(part).wait()


def local(images, texts, logit_scale, logit_bias):
    bf, f32 = jnp.bfloat16, jnp.float32
    dma = pltpu.SemaphoreType.DMA
    return pl.pallas_call(
        kernel,
        out_shape=(
            jax.ShapeDtypeStruct((IMG, D), f32),
            jax.ShapeDtypeStruct((TXT, D), f32),
        ),
        in_specs=[pl.BlockSpec(memory_space=pl.ANY)] * 4,
        out_specs=[pl.BlockSpec(memory_space=pl.ANY)] * 2,
        scratch_shapes=[
            pltpu.SMEM((1,), f32),
            pltpu.SMEM((1,), f32),
            pltpu.VMEM((IMG, D), bf),
            pltpu.VMEM((TXT, D), bf),
            pltpu.VMEM((NI * IMG, D), bf),
            pltpu.VMEM((9, TXT, D), bf),
            pltpu.VMEM((NI * IMG, D), f32),
            pltpu.VMEM((7, TXT, D), f32),
            pltpu.VMEM((NI * IMG, D), bf),
            pltpu.VMEM((NI * IMG, D), bf),
            pltpu.VMEM((3, TXT, D), bf),
            pltpu.VMEM((7, TXT, D), bf),
            pltpu.VMEM((3, TXT, D), bf),
            pltpu.VMEM((3, TXT, D), bf),
            pltpu.VMEM((IMG, D), f32),
            pltpu.VMEM((TXT, D), f32),
            dma((4,)), dma((1 + PARTS,)),
            dma((NI,)), dma((NI,)),
            dma((8, PARTS)), dma((9, PARTS)),
            dma((NI,)), dma((NI,)),
            dma((5, PARTS)), dma((7, PARTS)),
            dma((3,)), dma((3,)),
        ],
        compiler_params=pltpu.CompilerParams(
            collective_id=0, has_side_effects=True, vmem_limit_bytes=48 << 20
        ),
        name="pair_gradients",
    )(logit_scale, logit_bias, images, texts)


def solution(mesh):
    return jax.shard_map(
        local,
        mesh=mesh,
        in_specs=(P(("outer", "inner"), None), P(("outer", "inner"), None), P(), P()),
        out_specs=(P(("outer", "inner"), None), P(("outer", "inner"), None)),
        check_vma=False,
    )
```

```python
import functools
import math

import jax
import jax.numpy as jnp
from jax import lax
from jax.experimental import pallas as pl
from jax.experimental.pallas import tpu as pltpu
from jax.sharding import PartitionSpec as P

MESH = pl.DeviceIdType.MESH
HALF = 3
D = 1152
IMG = 16
TXT = 128
NO, NI = 32, 24
NZ = 12

STAGE_Z = ((0, 1, -1, 2, -2), (3, -3, 4, -4), (5, -5, 6))
STAGES = tuple(tuple((dz, dy) for dy in (0, 1) for dz in zs) for zs in STAGE_Z)
SLOTS = tuple(slot for stage in STAGES for slot in stage)
INDEX = {slot: n for n, slot in enumerate(SLOTS)}
STAGE_AT = (0, 10, 18, 24)
LATE_SLOTS = ((3, 0), (-3, 0))
PARTS = 4
HALVES = 2
PART = TXT // PARTS


def sign(value):
    return (value > 0) - (value < 0)


def gather_parent(slot):
    dz, dy = slot
    if dz == 0:
        return (0, 0)
    if dz == 6:
        return (4, 0) if dy == 0 else (-4, 1)
    if dz in (2, -2):
        return (0, 0)
    return (sign(dz) * ((abs(dz) - 1) // 2 * 2), dy)


def return_parent(slot):
    dz, dy = slot
    if dz == 6:
        return (3, 0) if dy == 0 else (-3, 0)
    if dy and abs(dz) < 5:
        return (dz, 0)
    return (sign(dz) * ((abs(dz) - 1) // 3 * 3), 0)


def kids_of(parent):
    return {
        slot: tuple(
            sorted((kid for kid in SLOTS[1:] if parent(kid) == slot), key=lambda kid: (kid[1] == slot[1], -abs(kid[0])))
        )
        for slot in SLOTS
    }


def move(start, end):
    dz = (end[0] - start[0]) % NZ
    return (dz - NZ if dz > NZ // 2 else dz, (end[1] - start[1]) % 2)


GATHER_KIDS = kids_of(gather_parent)
RETURN_KIDS = kids_of(return_parent)
MOVES = sorted(
    {move(gather_parent(slot), slot) for slot in SLOTS[1:]}
    | {move(slot, gather_parent(slot)) for slot in SLOTS[1:]}
)


def unit_rows(values):
    widened = values.astype(jnp.float32)
    inverse = lax.rsqrt(jnp.sum(widened * widened, axis=-1, keepdims=True) + 1e-06)
    return inverse, widened * inverse


def project_back(inverse, unit_full, gradient):
    along = jnp.sum(unit_full * gradient, axis=-1, keepdims=True)
    return inverse * (gradient - unit_full * along)


def kernel(
    scale_hbm, bias_hbm, img_hbm, txt_hbm, gi_hbm, gt_hbm,
    scale, bias, img_in, txt_in, img, txt, img_acc, txt_acc,
    i_send, i_recv, g_send, g_recv, p_send, p_recv, gi, gt, inv_img, inv_txt,
    in_sem, out_sem, ag_ss, ag_rs, t_ss, t_rs, i_ss, i_rs, g_ss, g_rs, p_ss, p_rs,
):
    o = lax.axis_index("outer")
    i = lax.axis_index("inner")
    core = o % 2
    x = (o // 2) % 4
    z = i // 2
    yl = i % 2
    divisor = 1.0 / math.sqrt((2 * HALF + 1) * NI * TXT)

    def along_z(dz, flip):
        return (o, ((z + dz + NZ) % NZ) * 2 + (1 - yl if flip else yl))

    def at(shift):
        return ((o + shift + NO) % NO, i)

    last_x = x // 3
    first_x = (3 - x) // 3
    last = last_x * yl
    first = first_x * yl
    through = last + first
    inner_end = last_x * core + first_x * (1 - core)
    outer_end = (x // 2) * (1 - x % 2) * core + (x % 2) * (1 - x // 2) * (1 - core)
    side = 2 * core - 1

    loads = [
        pltpu.make_async_copy(source, target, in_sem.at[n])
        for n, (source, target) in enumerate(
            ((img_hbm, img_in), (txt_hbm, txt_in), (scale_hbm, scale), (bias_hbm, bias))
        )
    ]
    for load in loads:
        load.start()

    barrier = pltpu.get_barrier_semaphore()

    def greet(device):
        pl.semaphore_signal(barrier, inc=1, device_id=device, device_id_type=MESH)

    peers = [along_z(dz, flip) for dz, flip in MOVES]
    peers += [at(1 - 2 * core), at(side), at(2), at(-2)]
    for peer in peers:
        greet(peer)

    @pl.when(through == 1)
    def _():
        greet(at(6 * first_x - 6 * last_x))
        greet(at(8))
        greet(at(-8))

    @pl.when(inner_end == 1)
    def _():
        greet(at(3 * side))
        greet(at(-5 * side))

    @pl.when(outer_end == 1)
    def _():
        greet(at(3 * side))
        greet(at(-5 * side))
        greet(at(8))
        greet(at(-8))

    loads[0].wait()
    inv_img[...], full = unit_rows(img_in[...])
    img[0:IMG, :] = full.astype(jnp.bfloat16)
    gi[...] = full

    pl.semaphore_wait(barrier, len(peers) + 3 * through + 2 * inner_end + 4 * outer_end)

    def gather_copy(kid):
        parent = gather_parent(kid)
        a, b = INDEX[parent], INDEX[kid]
        return pltpu.make_async_remote_copy(
            src_ref=img.at[a * IMG:(a + 1) * IMG],
            dst_ref=img.at[b * IMG:(b + 1) * IMG],
            send_sem=ag_ss.at[b],
            recv_sem=ag_rs.at[b],
            device_id=along_z(*move(parent, kid)),
            device_id_type=MESH,
        )

    def pass_on(slot):
        if slot != (0, 0):
            gather_copy(slot).wait_recv()
        for kid in GATHER_KIDS[slot]:
            gather_copy(kid).start()

    def text_copy(source, slot, n, device, part, parts):
        rows = pl.ds(part * (TXT // parts), TXT // parts)
        return pltpu.make_async_remote_copy(
            src_ref=txt.at[source, rows],
            dst_ref=txt.at[slot, rows],
            send_sem=t_ss.at[n, part],
            recv_sem=t_rs.at[slot, part],
            device_id=device,
            device_id_type=MESH,
        )

    def text_copies(source, slot, n, device, parts):
        return [text_copy(source, slot, n, device, part, parts) for part in range(parts)]

    partner = at(1 - 2 * core)
    up = at(2 - 8 * last)
    down = at(8 * first - 2)
    text_partner = text_copies(0, 1, 1, partner, 1)
    text_up = text_copies(0, 2 + 5 * last, 2, up, PARTS)
    text_down = text_copies(0, 3 + 5 * first, 3, down, PARTS)
    text_four = text_copies(2, 4, 4, partner, HALVES)
    text_five = text_copies(3, 5, 5, partner, HALVES)
    text_far = text_copies(3 - core, 6, 6, at(side), HALVES)
    text_far_own = text_copies(0, 6, 0, at(3 * side), HALVES)
    text_through = text_copies(7 + last, 2 + last, 7, at(8 * first - 8 * last), PARTS)

    def text_arrived(slot, part, parts):
        text_copy(0, slot, 0, partner, part, parts).wait_recv()

    def all_arrived(slot, parts):
        for part in range(parts):
            text_arrived(slot, part, parts)

    pass_on((0, 0))
    loads[1].wait()
    inv_txt[...], full = unit_rows(txt_in[...])
    txt[0] = full.astype(jnp.bfloat16)
    gt[...] = full
    for part in range(PARTS):
        text_up[part].start()
        text_down[part].start()

    @pl.when(outer_end == 1)
    def _():
        for part in range(HALVES):
            text_far_own[part].start()

    text_partner[0].start()
    pass_on((0, 1))
    loads[2].wait()
    loads[3].wait()
    factor = scale[0]
    offset = bias[0]

    def tile(first_stage, last_stage, slots, first_rows, first_cols):
        r0, r1 = STAGE_AT[first_stage] * IMG, STAGE_AT[last_stage + 1] * IMG
        s0, n = slots[0], len(slots)
        rows = img[r0:r1, :]
        cols = txt[s0:s0 + n].reshape(n * TXT, D)
        logits = lax.dot_general(
            cols, rows, (((1,), (1,)), ((), ())), preferred_element_type=jnp.float32
        ) * factor + offset
        if r0 == 0 and s0 == 0:
            shape = (n * TXT, r1 - r0)
            t = lax.broadcasted_iota(jnp.int32, shape, 0)
            r = lax.broadcasted_iota(jnp.int32, shape, 1)
            matched = jnp.logical_and(r == t, r < IMG)
            label = jnp.where(matched, 1.0, -1.0)
            weights = -label / (1.0 + jnp.exp(label * logits)) * divisor
        else:
            weights = divisor / (1.0 + jnp.exp(-logits))
        weights = weights.astype(jnp.bfloat16)
        text_part = jnp.dot(weights, rows, preferred_element_type=jnp.float32).reshape(n, TXT, D)
        image_part = lax.dot_general(
            weights, cols, (((0,), (0,)), ((), ())), preferred_element_type=jnp.float32
        )
        if first_rows:
            img_acc[r0:r1, :] = image_part
        else:
            img_acc[r0:r1, :] += image_part
        if first_cols:
            txt_acc[s0:s0 + n] = text_part
        else:
            txt_acc[s0:s0 + n] += text_part

    for slot in ((2, 0), (-2, 0), (2, 1), (-2, 1)):
        pass_on(slot)

    @pl.when(through == 1)
    def _():
        for part in range(PARTS):
            text_arrived(7 + last, part, PARTS)
            text_through[part].start()

    for slot in ((1, 0), (-1, 0), (1, 1), (-1, 1)):
        pass_on(slot)
    all_arrived(1, 1)
    tile(0, 0, (0, 1), True, True)
    for slot in ((4, 0), (-4, 0), (4, 1), (-4, 1)):
        pass_on(slot)
    for half in range(HALVES):
        for part in range(half * PARTS // HALVES, (half + 1) * PARTS // HALVES):
            text_arrived(2, part, PARTS)
            text_arrived(3, part, PARTS)

        @pl.when(inner_end == 0)
        def _():
            text_far[half].start()

        text_four[half].start()
        text_five[half].start()
    tile(0, 0, (2, 3), False, True)
    for slot in ((3, 0), (-3, 0), (3, 1), (-3, 1)):
        pass_on(slot)
    tile(1, 1, (0, 1, 2, 3), True, False)
    all_arrived(4, HALVES)
    all_arrived(5, HALVES)
    all_arrived(6, HALVES)
    tile(0, 1, (4, 5, 6), False, True)

    def grad_copy(source, slot, n, device, part, parts):
        rows = pl.ds(part * (TXT // parts), TXT // parts)
        return pltpu.make_async_remote_copy(
            src_ref=source.at[rows],
            dst_ref=g_recv.at[slot, rows],
            send_sem=g_ss.at[n, part],
            recv_sem=g_rs.at[slot, part],
            device_id=device,
            device_id_type=MESH,
        )

    def grad_copies(source, slot, n, device, parts):
        return [grad_copy(source, slot, n, device, part, parts) for part in range(parts)]

    def pair_copy(n):
        return pltpu.make_async_remote_copy(
            src_ref=p_send.at[n],
            dst_ref=p_recv.at[n],
            send_sem=p_ss.at[n],
            recv_sem=p_rs.at[n],
            device_id=partner,
            device_id_type=MESH,
        )

    far_shift = side * (1 - inner_end) - 5 * side * inner_end
    early_shift = core * (2 - 8 * last) + (1 - core) * (8 * first - 2)
    late_shift = (1 - core) * (2 - 8 * last) + core * (8 * first - 2)
    early_slot = core * 3 * last + (1 - core) * (1 + 3 * first)
    late_slot = (1 - core) * 3 * last + core * (1 + 3 * first)
    grad_far = grad_copies(g_send.at[2], 2 + 4 * inner_end, 2, at(far_shift), HALVES)
    grad_early = grad_copies(g_send.at[0], early_slot, 0, at(early_shift), PARTS)
    grad_late = grad_copies(g_send.at[1], late_slot, 1, at(late_shift), PARTS)
    grad_through = grad_copies(g_recv.at[3 + last], last, 3, at(8 * first - 8 * last), PARTS)
    grad_far_through = grad_copies(g_recv.at[6], 5, 4, at(-8 * side), HALVES)
    pair_own, pair_early, pair_late = pair_copy(0), pair_copy(2 - core), pair_copy(1 + core)

    def grad_arrived(slot, part, parts=PARTS):
        grad_copy(g_send.at[0], slot, 0, partner, part, parts).wait_recv()

    def pair_arrived(n):
        pair_copy(n).wait_recv()

    def image_copy(slot):
        rows = pl.ds(INDEX[slot] * IMG, IMG)
        return pltpu.make_async_remote_copy(
            src_ref=i_send.at[rows],
            dst_ref=i_recv.at[rows],
            send_sem=i_ss.at[INDEX[slot]],
            recv_sem=i_rs.at[INDEX[slot]],
            device_id=along_z(*move(slot, return_parent(slot))),
            device_id_type=MESH,
        )

    def image_sum(slot):
        total = img_acc[pl.ds(INDEX[slot] * IMG, IMG), :]
        for kid in RETURN_KIDS[slot]:
            image_copy(kid).wait_recv()
            total = total + i_recv[pl.ds(INDEX[kid] * IMG, IMG), :].astype(jnp.float32)
        return total

    def give_back(*slots):
        for slot in slots:
            i_send[pl.ds(INDEX[slot] * IMG, IMG), :] = image_sum(slot).astype(jnp.bfloat16)
            image_copy(slot).start()

    give_back((0, 1), (4, 1), (-4, 1), (3, 1), (-3, 1), (2, 1), (-2, 1), (1, 1), (-1, 1))
    for slot in STAGES[2]:
        pass_on(slot)
    tile(2, 2, (4, 5, 6), True, False)
    g_send[2] = txt_acc[6].astype(jnp.bfloat16)
    for copy in grad_far:
        copy.start()
    p_send[2 - core] = txt_acc[5 - core].astype(jnp.bfloat16)
    pair_early.start()
    p_send[1 + core] = txt_acc[4 + core].astype(jnp.bfloat16)
    pair_late.start()
    tile(2, 2, (0, 1, 2, 3), False, False)
    give_back((6, 0), (6, 1), (5, 1), (-5, 1), (5, 0), (-5, 0), (4, 0), (-4, 0))
    pair_arrived(1 + core)
    for part in range(PARTS):
        rows = pl.ds(part * PART, PART)
        g_send[0, rows] = (txt_acc[2 + core, rows] + p_recv[1 + core, rows].astype(jnp.float32)).astype(jnp.bfloat16)
        grad_early[part].start()
    p_send[0] = txt_acc[1].astype(jnp.bfloat16)
    pair_own.start()
    give_back((2, 0), (-2, 0), (1, 0), (-1, 0))

    pair_arrived(2 - core)
    for part in range(PARTS):
        rows = pl.ds(part * PART, PART)

        @pl.when(inner_end == 0)
        def _():
            if part % (PARTS // HALVES) == 0:
                grad_arrived(2, part * HALVES // PARTS, HALVES)
            g_send[1, rows] = (
                txt_acc[3 - core, rows]
                + p_recv[2 - core, rows].astype(jnp.float32)
                + g_recv[2, rows].astype(jnp.float32)
            ).astype(jnp.bfloat16)

        @pl.when(inner_end == 1)
        def _():
            g_send[1, rows] = (
                txt_acc[3 - core, rows] + p_recv[2 - core, rows].astype(jnp.float32)
            ).astype(jnp.bfloat16)

        grad_late[part].start()

    give_back((3, 0), (-3, 0))

    @pl.when(outer_end == 1)
    def _():
        for part in range(HALVES):
            grad_arrived(6, part, HALVES)
            grad_far_through[part].start()

    def go_through():
        for part in range(PARTS):
            grad_arrived(3 + last, part)
            grad_through[part].start()

    early_through = first * core + last * (1 - core)
    late_through = first * (1 - core) + last * core

    @pl.when(early_through == 1)
    def _():
        go_through()


    @pl.when(late_through == 1)
    def _():
        go_through()

    for slot in SLOTS[1:]:
        gather_copy(slot).wait_send()
        if slot not in LATE_SLOTS:
            image_copy(slot).wait_send()
    for copy in (pair_own, pair_early, pair_late):
        copy.wait_send()
    for copies in (text_partner, text_up, text_down, text_four, text_five, grad_far, grad_early):
        for copy in copies:
            copy.wait_send()

    @pl.when(inner_end == 0)
    def _():
        for copy in text_far:
            copy.wait_send()

    @pl.when(outer_end == 1)
    def _():
        for copy in text_far_own:
            copy.wait_send()

    @pl.when(through == 1)
    def _():
        for copy in text_through:
            copy.wait_send()

    gi[...] = project_back(inv_img[...], gi[...], image_sum((0, 0)) * factor)
    store_img = pltpu.make_async_copy(gi, gi_hbm, out_sem.at[0])
    store_img.start()

    def store_txt(part):
        rows = pl.ds(part * PART, PART)
        return pltpu.make_async_copy(gt.at[rows], gt_hbm.at[rows], out_sem.at[1 + part])

    pair_arrived(0)
    for part in range(PARTS):
        rows = pl.ds(part * PART, PART)
        grad_arrived(0, part)
        grad_arrived(1, part)
        txt_acc[0, rows] += p_recv[0, rows].astype(jnp.float32) + (
            g_recv[0, rows].astype(jnp.float32) + g_recv[1, rows].astype(jnp.float32)
        )

        @pl.when(outer_end == 1)
        def _():
            if part % (PARTS // HALVES) == 0:
                grad_arrived(5, part * HALVES // PARTS, HALVES)
            txt_acc[0, rows] += g_recv[5, rows].astype(jnp.float32)

        gt[rows, :] = project_back(inv_txt[rows, :], gt[rows, :], txt_acc[0, rows] * factor)
        store_txt(part).start()

    for slot in LATE_SLOTS:
        image_copy(slot).wait_send()
    for copy in grad_late:
        copy.wait_send()

    @pl.when(outer_end == 1)
    def _():
        for copy in grad_far_through:
            copy.wait_send()

    @pl.when(through == 1)
    def _():
        for copy in grad_through:
            copy.wait_send()

    store_img.wait()
    for part in range(PARTS):
        store_txt(part).wait()


def local(images, texts, logit_scale, logit_bias):
    bf, f32 = jnp.bfloat16, jnp.float32
    dma = pltpu.SemaphoreType.DMA
    return pl.pallas_call(
        kernel,
        out_shape=(
            jax.ShapeDtypeStruct((IMG, D), f32),
            jax.ShapeDtypeStruct((TXT, D), f32),
        ),
        in_specs=[pl.BlockSpec(memory_space=pl.ANY)] * 4,
        out_specs=[pl.BlockSpec(memory_space=pl.ANY)] * 2,
        scratch_shapes=[
            pltpu.SMEM((1,), f32),
            pltpu.SMEM((1,), f32),
            pltpu.VMEM((IMG, D), bf),
            pltpu.VMEM((TXT, D), bf),
            pltpu.VMEM((NI * IMG, D), bf),
            pltpu.VMEM((9, TXT, D), bf),
            pltpu.VMEM((NI * IMG, D), f32),
            pltpu.VMEM((7, TXT, D), f32),
            pltpu.VMEM((NI * IMG, D), bf),
            pltpu.VMEM((NI * IMG, D), bf),
            pltpu.VMEM((3, TXT, D), bf),
            pltpu.VMEM((7, TXT, D), bf),
            pltpu.VMEM((3, TXT, D), bf),
            pltpu.VMEM((3, TXT, D), bf),
            pltpu.VMEM((IMG, D), f32),
            pltpu.VMEM((TXT, D), f32),
            pltpu.VMEM((IMG, 1), f32),
            pltpu.VMEM((TXT, 1), f32),
            dma((4,)), dma((1 + PARTS,)),
            dma((NI,)), dma((NI,)),
            dma((8, PARTS)), dma((9, PARTS)),
            dma((NI,)), dma((NI,)),
            dma((5, PARTS)), dma((7, PARTS)),
            dma((3,)), dma((3,)),
        ],
        compiler_params=pltpu.CompilerParams(
            collective_id=0, has_side_effects=True, vmem_limit_bytes=48 << 20
        ),
        name="pair_gradients",
    )(logit_scale, logit_bias, images, texts)


def solution(mesh):
    return jax.shard_map(
        local,
        mesh=mesh,
        in_specs=(P(("outer", "inner"), None), P(("outer", "inner"), None), P(), P()),
        out_specs=(P(("outer", "inner"), None), P(("outer", "inner"), None)),
        check_vma=False,
    )
```
